32 devices in a mesh: section: 2 (over core), ctx: 4 (over z), fsdp: 4 (over y, x).
Axes of the slice: x: 2, y: 2, z: 4, core: 2. Of those that a mesh axis runs over, the one named last changes fastest.
Arguments:
- block_input: bfloat16 [1, 4, 512, 576], P(None, 'fsdp', 'ctx'), may hold values from -6 to 6
- cotangent: bfloat16 [1, 4, 512, 576], P(None, 'fsdp', 'ctx'), may hold values from -6 to 6
- span_order: int32 [8], replicated, may hold values from 0 to 7, as said below
- rope_ids: int32 [1, 4, 512], P(None, 'fsdp', 'ctx'), may hold values from 0 to 511, as said below
- norm_in: float32 [2, 576], P('section'), may hold values from 0.5 to 1.5
- w_query: bfloat16 [2, 576, 576], P('section', 'fsdp'), may hold values from -0.25 to 0.25
- w_key: bfloat16 [2, 576, 192], P('section', 'fsdp'), may hold values from -0.25 to 0.25
- w_value: bfloat16 [2, 576, 192], P('section', 'fsdp'), may hold values from -0.25 to 0.25
- w_out: bfloat16 [2, 576, 576], P('section', 'fsdp'), may hold values from -2 to 2
- norm_mid: float32 [2, 576], P('section'), may hold values from 0.5 to 1.5
- w_gate: bfloat16 [2, 576, 1536], P('section', 'fsdp'), may hold values from -0.25 to 0.25
- w_up: bfloat16 [2, 576, 1536], P('section', 'fsdp'), may hold values from -0.25 to 0.25
- w_down: bfloat16 [2, 1536, 576], P('section', 'fsdp'), may hold values from -0.15625 to 0.15625
Outputs:
- layer_out: bfloat16 [2, 1, 4, 512, 576], P('section', None, 'fsdp', 'ctx')
- grad_in: float32 [2, 1, 4, 512, 576], P('section', None, 'fsdp', 'ctx')
- grad_norm_in: float32 [2, 576], P('section', 'fsdp')
- grad_query: float32 [2, 576, 576], P('section', 'fsdp')
- grad_key: float32 [2, 576, 192], P('section', 'fsdp')
- grad_value: float32 [2, 576, 192], P('section', 'fsdp')
- grad_out: float32 [2, 576, 576], P('section', 'fsdp')
- grad_norm_mid: float32 [2, 576], P('section', 'fsdp')
- grad_gate: float32 [2, 576, 1536], P('section', 'fsdp')
- grad_up: float32 [2, 576, 1536], P('section', 'fsdp')
- grad_down: float32 [2, 1536, 576], P('section', 'fsdp')
The draws below stay inside these ranges and needn't reach their ends.
Inputs may be any that keep to these rules, and one draw needn't show every extreme that they name: The rows of every sequence are stored span after span: index c of ctx holds span span_order[2 c] then span span_order[2 c + 1], each of 64 consecutive positions; every span appears once, and the two spans of one index are i and (the number of spans) - 1 - i for some i. `rope_ids`: A token's position minus that of the first token of its packed document; documents follow one another without gaps; the first sequence of every micro-batch is a single document.
All inputs are finite; a program needn't handle non-finite values.
Results may differ from the reference program's by a relative error of at most 0.023.
Values may be sent and summed in bfloat16 or wider, within the bound.
A program may use at most 128 MiB of HBM per device.

```python
import math
import jax
import jax.numpy as jnp
from jax import lax

D = 576
HEADS = 9
KV_HEADS = 3
HEAD = 64
FF = 1536
SPAN = 64
MICRO = 1
SEQ_LEN = 512
SEQS = 4
N_CTX = 4


def mirrored_order(key):
    base = jax.random.fold_in(key, 11)
    pairs = jax.random.permutation(jax.random.fold_in(base, 1), N_CTX).astype(jnp.int32)
    flips = jax.random.randint(jax.random.fold_in(base, 2), (N_CTX,), 0, 2)
    mirror = 2 * N_CTX - 1 - pairs
    front = jnp.where(flips == 1, mirror, pairs)
    behind = jnp.where(flips == 1, pairs, mirror)
    return jnp.stack([front, behind], axis=1).reshape(2 * N_CTX).astype(jnp.int32)


def draw_span_order(key, part):
    return mirrored_order(key)


def draw_rope_ids(key, part):
    order = mirrored_order(key)
    row_ids = jnp.arange(SEQ_LEN, dtype=jnp.int32)
    slot_of = 2 * (row_ids // (2 * SPAN)) + row_ids % (2 * SPAN) // SPAN
    stored = order[slot_of] * SPAN + row_ids % SPAN
    marks = jax.random.randint(jax.random.fold_in(key, 23), (MICRO, SEQS, SEQ_LEN), 0, 1024) == 0
    seq_ids = jnp.arange(SEQS, dtype=jnp.int32)[None, :, None]
    places = jnp.arange(SEQ_LEN, dtype=jnp.int32)[None, None, :]
    starts = jnp.where(marks & (seq_ids > 0) | (places == 0), places, 0)
    starts = lax.cummax(starts, axis=2)
    within = places - starts
    return within[:, :, stored].astype(jnp.int32)


def block_scale(key, shape, shards, least, high):
    def one(axis_at, shards_of):
        draws = jax.random.uniform(jax.random.fold_in(jax.random.fold_in(key, 6), axis_at), (shards_of,), jnp.float32, least / len(shards), high / len(shards))
        return jnp.repeat(jnp.exp(draws), shape[axis_at] // shards_of).reshape((-1,) + (1,) * (len(shape) - axis_at - 1))

    loudness = one(*shards[0])
    for cut in shards[1:]:
        loudness = loudness * one(*cut)
    return loudness


def normal_values(key, dims, scale, most, split=(), kind=jnp.bfloat16):
    loudness = block_scale(key, dims, split, -0.22, 0.18) if split else 1.0
    entries = jax.random.normal(key, dims, jnp.float32) * scale * loudness
    return jnp.minimum(jnp.maximum(entries, -most), most).astype(kind)


def setup_inputs(seed: int = 0) -> dict:
    splits = jax.random.split(jax.random.key(seed), 14)
    return {
        "block_input": normal_values(splits[0], (MICRO, SEQS, SEQ_LEN, D), 1.0, 6.0, ((1, 4), (2, 4))),
        "cotangent": normal_values(splits[1], (MICRO, SEQS, SEQ_LEN, D), 1.0, 6.0, ((1, 4), (2, 4))),
        "span_order": draw_span_order(jax.random.fold_in(splits[13], 71), 0),
        "rope_ids": draw_rope_ids(jax.random.fold_in(splits[13], 71), 0),
        "norm_in": jnp.clip(1.0 + 0.1 * jax.random.normal(splits[4], (2, D), jnp.float32), 0.5, 1.5),
        "w_query": normal_values(splits[5], (2, D, HEADS * HEAD), D ** -0.5, 0.25, ((0, 2), (1, 4))),
        "w_key": normal_values(splits[6], (2, D, KV_HEADS * HEAD), D ** -0.5, 0.25, ((0, 2), (1, 4))),
        "w_value": normal_values(splits[7], (2, D, KV_HEADS * HEAD), D ** -0.5, 0.25, ((0, 2), (1, 4))),
        "w_out": normal_values(splits[8], (2, HEADS * HEAD, D), (max(HEADS * HEAD // 64, 4)) ** -0.5, 2.0, ((0, 2), (1, 4))),
        "norm_mid": jnp.clip(1.0 + 0.1 * jax.random.normal(splits[9], (2, D), jnp.float32), 0.5, 1.5),
        "w_gate": normal_values(splits[10], (2, D, FF), D ** -0.5, 0.25, ((0, 2), (1, 4))),
        "w_up": normal_values(splits[11], (2, D, FF), D ** -0.5, 0.25, ((0, 2), (1, 4))),
        "w_down": normal_values(splits[12], (2, FF, D), FF ** -0.5, 0.15625, ((0, 2), (1, 4))),
    }


EPS = 1e-05
THETA = 100000.0

def stored_positions(span_order):
    row_ids = jnp.arange(SEQ_LEN, dtype=jnp.int32)
    slot_of = (2 * (row_ids // (2 * SPAN)) + row_ids % (2 * SPAN) // SPAN).astype(jnp.int32)
    return (span_order[slot_of] * SPAN + row_ids % SPAN).astype(jnp.int32)

def rope_tables(rope_rows):
    half_width = HEAD // 2
    frequency = THETA ** (-jnp.arange(half_width, dtype=jnp.float32) * (2.0 / HEAD))
    angle = rope_rows.astype(jnp.float32)[:, None] * frequency[None, :]
    return (jnp.cos(angle), jnp.sin(angle))

def rotate(vectors, cosine, sine):
    half_width = vectors.shape[-1] // 2
    front = vectors[..., :half_width]
    second = vectors[..., half_width:]
    cos_rows = cosine[:, None, :]
    sin_rows = sine[:, None, :]
    return jnp.concatenate([front * cos_rows - second * sin_rows, second * cos_rows + front * sin_rows], axis=-1)

def normalize(field):
    factor = lax.rsqrt(lax.optimization_barrier(jnp.mean(field * field, axis=-1, keepdims=True)) + EPS)
    return (field * factor, factor)

def norm_back(grad_rows, normed, factor, gain):
    scaled = grad_rows * gain
    back = factor * (scaled - normed * lax.optimization_barrier(jnp.mean(scaled * normed, axis=-1, keepdims=True)))
    return (back, lax.optimization_barrier(jnp.sum(grad_rows * normed, axis=0)))

def attend_all(queries, kv_all, positions):
    width = kv_all.shape[1] // 2
    key_heads = kv_all[:, :width].reshape(SEQ_LEN, KV_HEADS, HEAD).astype(jnp.float32)
    value_heads = kv_all[:, width:].reshape(SEQ_LEN, KV_HEADS, HEAD).astype(jnp.float32)
    block_rows = math.gcd(SEQ_LEN, 512)
    blocks = SEQ_LEN // block_rows
    score_scale = HEAD ** (-0.5)

    def per_block(args):
        query_block, pos_block = args
        scores = jnp.einsum('rkgd,lkd->rkgl', query_block.astype(jnp.float32), key_heads) * score_scale
        allowed = positions[None, :] <= pos_block[:, None]
        scores = jnp.where(allowed[:, None, None, :], scores, -jnp.inf)
        row_top = lax.optimization_barrier(jnp.max(scores, axis=-1, keepdims=True))
        log_total = row_top[..., 0] + jnp.log(lax.optimization_barrier(jnp.sum(jnp.exp(scores - row_top), axis=-1)))
        probs = lax.optimization_barrier(jnp.exp(scores - log_total[..., None]).astype(jnp.bfloat16))
        attended = jnp.einsum('rkgl,lkd->rkgd', probs.astype(jnp.float32), value_heads).astype(jnp.bfloat16)
        return (attended, log_total)
    shaped = queries.reshape(blocks, block_rows, KV_HEADS, HEADS // KV_HEADS, HEAD)
    attended, log_total = lax.map(per_block, (shaped, positions.reshape(blocks, block_rows)))
    return (attended.reshape(queries.shape), log_total.reshape(queries.shape[:3]))

def attend_back(queries, kv_all, positions, log_total, grad_att, row_delta):
    width = kv_all.shape[1] // 2
    key_heads = kv_all[:, :width].reshape(SEQ_LEN, KV_HEADS, HEAD).astype(jnp.float32)
    value_heads = kv_all[:, width:].reshape(SEQ_LEN, KV_HEADS, HEAD).astype(jnp.float32)
    block_rows = math.gcd(SEQ_LEN, 512)
    blocks = SEQ_LEN // block_rows
    score_scale = HEAD ** (-0.5)
    group = HEADS // KV_HEADS

    def per_block(running, args):
        query_block, pos_block, total_block, grad_block, delta_block = args
        query_f = query_block.astype(jnp.float32)
        grad_f = grad_block.astype(jnp.float32)
        scores = jnp.einsum('rkgd,lkd->rkgl', query_f, key_heads) * score_scale
        allowed = positions[None, :] <= pos_block[:, None]
        scores = jnp.where(allowed[:, None, None, :], scores, -jnp.inf)
        probs = jnp.exp(scores - total_block[..., None])
        probs_b = lax.optimization_barrier(probs.astype(jnp.bfloat16)).astype(jnp.float32)
        grad_v = jnp.einsum('rkgl,rkgd->lkd', probs_b, grad_f)
        grad_p = jnp.einsum('rkgd,lkd->rkgl', grad_f, value_heads)
        grad_s = lax.optimization_barrier((probs * (grad_p - delta_block[..., None])).astype(jnp.bfloat16)).astype(jnp.float32)
        grad_q = jnp.einsum('rkgl,lkd->rkgd', grad_s, key_heads) * score_scale
        grad_k = jnp.einsum('rkgl,rkgd->lkd', grad_s, query_f) * score_scale
        running = running + jnp.concatenate([grad_k.reshape(SEQ_LEN, width), grad_v.reshape(SEQ_LEN, width)], axis=1)
        return (running, grad_q)
    shape_b = (blocks, block_rows, KV_HEADS, group, HEAD)
    inputs_b = (queries.reshape(shape_b), positions.reshape(blocks, block_rows), log_total.reshape(blocks, block_rows, KV_HEADS, group), grad_att.reshape(shape_b), row_delta.reshape(blocks, block_rows, KV_HEADS, group))
    grad_kv, grad_q = lax.scan(per_block, jnp.zeros((SEQ_LEN, 2 * width), jnp.float32), inputs_b)
    return (grad_q.reshape(queries.shape), grad_kv)

def layer_forward(layer_input, rope_rows, positions, params):
    gain_in, w_q, w_k, w_v, w_o, gain_mid, w_g, w_u, w_d = params
    residual = layer_input.astype(jnp.float32)
    normed_in, scale_in = normalize(residual)
    hidden_in = (normed_in * gain_in).astype(jnp.bfloat16)
    cosine, sine = rope_tables(rope_rows)
    query = jnp.dot(hidden_in, w_q, preferred_element_type=jnp.float32).reshape(SEQ_LEN, HEADS, HEAD)
    key_proj = jnp.dot(hidden_in, w_k, preferred_element_type=jnp.float32).reshape(SEQ_LEN, KV_HEADS, HEAD)
    value = jnp.dot(hidden_in, w_v, preferred_element_type=jnp.float32).astype(jnp.bfloat16)
    query_b = rotate(query, cosine, sine).astype(jnp.bfloat16).reshape(SEQ_LEN, KV_HEADS, HEADS // KV_HEADS, HEAD)
    key_b = rotate(key_proj, cosine, sine).astype(jnp.bfloat16).reshape(SEQ_LEN, KV_HEADS * HEAD)
    kv_all = jnp.concatenate([key_b, value], axis=1)
    attended, log_total = attend_all(query_b, kv_all, positions)
    attended_flat = attended.reshape(SEQ_LEN, HEADS * HEAD)
    residual_mid = residual + jnp.dot(attended_flat, w_o, preferred_element_type=jnp.float32)
    normed_mid, scale_mid = normalize(residual_mid)
    hidden_mid = (normed_mid * gain_mid).astype(jnp.bfloat16)
    gate_pre = jnp.dot(hidden_mid, w_g, preferred_element_type=jnp.float32)
    up_pre = jnp.dot(hidden_mid, w_u, preferred_element_type=jnp.float32)
    active = (jax.nn.silu(gate_pre) * up_pre).astype(jnp.bfloat16)
    result = residual_mid + jnp.dot(active, w_d, preferred_element_type=jnp.float32)
    saved = (normed_in, scale_in, hidden_in, cosine, sine, query_b, kv_all, attended, log_total, normed_mid, scale_mid, hidden_mid, gate_pre, up_pre, active)
    return (result, saved)

def layer_backward(saved, params, positions, grad_y):
    gain_in, w_q, w_k, w_v, w_o, gain_mid, w_g, w_u, w_d = params
    normed_in, scale_in, hidden_in, cosine, sine, query_b, kv_all, attended, log_total, normed_mid, scale_mid, hidden_mid, gate_pre, up_pre, active = saved
    grad_yb = grad_y.astype(jnp.bfloat16)
    grad_wd = jnp.dot(active.T, grad_yb, preferred_element_type=jnp.float32)
    grad_act = jnp.dot(grad_yb, w_d.T, preferred_element_type=jnp.float32)
    sigmoid_gate = jax.nn.sigmoid(gate_pre)
    grad_gate = (grad_act * up_pre * sigmoid_gate * (1.0 + gate_pre * (1.0 - sigmoid_gate))).astype(jnp.bfloat16)
    grad_up = (grad_act * gate_pre * sigmoid_gate).astype(jnp.bfloat16)
    grad_wg = jnp.dot(hidden_mid.T, grad_gate, preferred_element_type=jnp.float32)
    grad_wu = jnp.dot(hidden_mid.T, grad_up, preferred_element_type=jnp.float32)
    grad_hmid = jnp.dot(grad_gate, w_g.T, preferred_element_type=jnp.float32) + jnp.dot(grad_up, w_u.T, preferred_element_type=jnp.float32)
    back_mid, grad_gmid = norm_back(grad_hmid, normed_mid, scale_mid, gain_mid)
    grad_mid = grad_y + back_mid
    grad_midb = grad_mid.astype(jnp.bfloat16)
    attended_flat = attended.reshape(SEQ_LEN, HEADS * HEAD)
    grad_wo = jnp.dot(attended_flat.T, grad_midb, preferred_element_type=jnp.float32)
    grad_att = jnp.dot(grad_midb, w_o.T, preferred_element_type=jnp.float32).astype(jnp.bfloat16).reshape(attended.shape)
    row_delta = lax.optimization_barrier(jnp.sum(grad_att.astype(jnp.float32) * attended.astype(jnp.float32), axis=-1))
    grad_q, grad_kv = attend_back(query_b, kv_all, positions, log_total, grad_att, row_delta)
    width = kv_all.shape[1] // 2
    grad_qraw = rotate(grad_q.reshape(SEQ_LEN, HEADS, HEAD), cosine, -sine).astype(jnp.bfloat16).reshape(SEQ_LEN, HEADS * HEAD)
    grad_kraw = rotate(grad_kv[:, :width].reshape(SEQ_LEN, KV_HEADS, HEAD), cosine, -sine).astype(jnp.bfloat16).reshape(SEQ_LEN, width)
    grad_vb = grad_kv[:, width:].astype(jnp.bfloat16)
    grad_wq = jnp.dot(hidden_in.T, grad_qraw, preferred_element_type=jnp.float32)
    grad_wk = jnp.dot(hidden_in.T, grad_kraw, preferred_element_type=jnp.float32)
    grad_wv = jnp.dot(hidden_in.T, grad_vb, preferred_element_type=jnp.float32)
    grad_hin = jnp.dot(grad_qraw, w_q.T, preferred_element_type=jnp.float32) + jnp.dot(grad_kraw, w_k.T, preferred_element_type=jnp.float32) + jnp.dot(grad_vb, w_v.T, preferred_element_type=jnp.float32)
    back_in, grad_gin = norm_back(grad_hin, normed_in, scale_in, gain_in)
    grad_entry = grad_mid + back_in
    return (grad_entry, (grad_gin, grad_wq, grad_wk, grad_wv, grad_wo, grad_gmid, grad_wg, grad_wu, grad_wd))

def reference(block_input, cotangent, span_order, rope_ids, norm_in, w_query, w_key, w_value, w_out, norm_mid, w_gate, w_up, w_down):
    positions = stored_positions(span_order)
    stacked = (norm_in, w_query, w_key, w_value, w_out, norm_mid, w_gate, w_up, w_down)
    layer_zero = tuple((weight[0] for weight in stacked))
    layer_one = tuple((weight[1] for weight in stacked))
    zeros_like = jax.tree.map(lambda weight: jnp.zeros(weight.shape[1:], jnp.float32), stacked)

    def one_sequence(running, args):
        sequence, grad_seq, rope_rows = args
        result_zero, saved_zero = layer_forward(sequence, rope_rows, positions, layer_zero)
        middle = lax.optimization_barrier(result_zero.astype(jnp.bfloat16))
        result_one, saved_one = layer_forward(middle, rope_rows, positions, layer_one)
        final = result_one.astype(jnp.bfloat16)
        grad_one, terms_one = layer_backward(saved_one, layer_one, positions, grad_seq.astype(jnp.float32))
        sent_back = lax.optimization_barrier(grad_one.astype(jnp.bfloat16))
        grad_zero, terms_zero = layer_backward(saved_zero, layer_zero, positions, sent_back.astype(jnp.float32))
        sums_zero, sums_one = running
        sums_zero = jax.tree.map(lambda left, right: left + right, sums_zero, terms_zero)
        sums_one = jax.tree.map(lambda left, right: left + right, sums_one, terms_one)
        return ((sums_zero, sums_one), (jnp.stack([middle, final]), jnp.stack([grad_zero, grad_one])))
    sequences = block_input.reshape(MICRO * SEQS, SEQ_LEN, D)
    grads_seq = cotangent.reshape(MICRO * SEQS, SEQ_LEN, D)
    rope_seq = rope_ids.reshape(MICRO * SEQS, SEQ_LEN)
    (sums_zero, sums_one), (outs_all, grads_all) = lax.scan(one_sequence, (zeros_like, zeros_like), (sequences, grads_seq, rope_seq))
    layer_out = jnp.transpose(outs_all, (1, 0, 2, 3)).reshape(2, MICRO, SEQS, SEQ_LEN, D)
    grad_in = jnp.transpose(grads_all, (1, 0, 2, 3)).reshape(2, MICRO, SEQS, SEQ_LEN, D)
    grads = tuple((jnp.stack([left, right]) for left, right in zip(sums_zero, sums_one)))
    return (layer_out, grad_in, grads[0], grads[1], grads[2], grads[3], grads[4], grads[5], grads[6], grads[7], grads[8])
```

```python
import functools
import math

import jax
import jax.numpy as jnp
from jax import lax
from jax.experimental import pallas as pl
from jax.experimental.pallas import tpu as pltpu
from jax.sharding import PartitionSpec as P

KV_HEADS = 3
HEAD = 64


EPS = 1e-05
THETA = 100000.0


LANES = 128
VMEM_BYTES = 48 * 1024 * 1024


def padded(width):
    return -(-width // LANES) * LANES


def greet(peers):
    barrier = pltpu.get_barrier_semaphore()
    for axis, place in peers:
        pl.semaphore_signal(
            barrier, inc=1, device_id={axis: place}, device_id_type=pl.DeviceIdType.MESH
        )
    pl.semaphore_wait(barrier, len(peers))


def push(source, target, send_sem, recv_sem, axis, place):
    return pltpu.make_async_remote_copy(
        src_ref=source,
        dst_ref=target,
        send_sem=send_sem,
        recv_sem=recv_sem,
        device_id={axis: place},
        device_id_type=pl.DeviceIdType.MESH,
    )


def call_options(collective_id):
    return pltpu.CompilerParams(
        collective_id=collective_id, has_side_effects=True, vmem_limit_bytes=VMEM_BYTES
    )


def spread_kernel(count, own_ref, all_ref, send_sem, recv_sem):
    me = lax.axis_index("ctx")
    greet([("ctx", lax.rem(me + step, count)) for step in range(1, count)])
    copies = []
    for step in range(1, count):
        copy = push(
            own_ref,
            all_ref.at[me],
            send_sem.at[step - 1],
            recv_sem.at[step - 1],
            "ctx",
            lax.rem(me + step, count),
        )
        copy.start()
        copies.append(copy)
    all_ref[me] = own_ref[...]
    for copy in copies:
        copy.wait()


def spread(own, collective_id):
    count = lax.axis_size("ctx")
    whole = pl.BlockSpec(memory_space=pltpu.VMEM)
    return pl.pallas_call(
        functools.partial(spread_kernel, count),
        out_shape=jax.ShapeDtypeStruct((count,) + own.shape, own.dtype),
        in_specs=[whole],
        out_specs=whole,
        scratch_shapes=[
            pltpu.SemaphoreType.DMA((count - 1,)),
            pltpu.SemaphoreType.DMA((count - 1,)),
        ],
        compiler_params=call_options(collective_id),
        name="spread",
    )(own).reshape((count * own.shape[0],) + own.shape[1:])


def collect_kernel(count, pieces_ref, sum_ref, packed, landed, send_sem, recv_sem):
    me = lax.axis_index("ctx")
    greet([("ctx", lax.rem(me + step, count)) for step in range(1, count)])
    copies = []
    for step in range(1, count):
        place = lax.rem(me + step, count)
        packed[step - 1] = pieces_ref[place].astype(jnp.bfloat16)
        copy = push(
            packed.at[step - 1],
            landed.at[step - 1],
            send_sem.at[step - 1],
            recv_sem.at[step - 1],
            "ctx",
            place,
        )
        copy.start()
        copies.append(copy)
    total = pieces_ref[me]
    for step, copy in enumerate(copies):
        copy.wait_recv()
        total = total + landed[step].astype(jnp.float32)
    sum_ref[...] = total
    for copy in copies:
        copy.wait_send()


def collect(pieces, collective_id):
    count = lax.axis_size("ctx")
    whole = pl.BlockSpec(memory_space=pltpu.VMEM)
    blocks = pieces.reshape((count, -1) + pieces.shape[1:])
    slots = (count - 1,) + blocks.shape[1:]
    return pl.pallas_call(
        functools.partial(collect_kernel, count),
        out_shape=jax.ShapeDtypeStruct(blocks.shape[1:], jnp.float32),
        in_specs=[whole],
        out_specs=whole,
        scratch_shapes=[
            pltpu.VMEM(slots, jnp.bfloat16),
            pltpu.VMEM(slots, jnp.bfloat16),
            pltpu.SemaphoreType.DMA((count - 1,)),
            pltpu.SemaphoreType.DMA((count - 1,)),
        ],
        compiler_params=call_options(collective_id),
        name="collect",
    )(blocks)


def grads_kernel(
    active,
    rows_f,
    count_c,
    part,
    products,
    hid_in,
    att,
    hid_mid,
    grad_y,
    d_qkv,
    d_mid,
    d_ff,
    act,
    gains,
    out,
    made,
    landed,
    summed,
    landed_c,
    total,
    send_f,
    recv_f,
    send_c,
    recv_c,
    send_g,
    recv_g,
):
    off_ff, off_down, off_gain, off_out, off_qkv, end = products
    f_place = lax.axis_index("fsdp")
    c_place = lax.axis_index("ctx")

    def put(block, offset, left, right):
        width = right.shape[1]
        for first in range(0, width, 512):
            size = min(512, width - first)
            made[block, :, pl.ds(offset + first, size)] = jnp.dot(
                left, right[:, first : first + size], preferred_element_type=jnp.float32
            ).astype(jnp.bfloat16)

    def compute(block):
        put(block, off_ff, hid_mid[block], d_ff[...])
        step_rows = act.shape[2]
        for index in range(rows_f):
            put(block, off_down + index * step_rows, grad_y[index], act[block])
        made[block, :, pl.ds(off_gain, LANES)] = gains[block]
        put(block, off_out, att[block], d_mid[...])
        put(block, off_qkv, hid_in[block], d_qkv[...])
        if end < count_c * part:
            made[block, :, pl.ds(end, count_c * part - end)] = jnp.zeros(
                (made.shape[1], count_c * part - end), jnp.bfloat16
            )

    def columns(index):
        return pl.ds(pl.multiple_of(index * part, LANES), part)

    @pl.when(lax.axis_index("section") == active)
    def run():
        f_peers = [lax.rem(f_place + step, rows_f) for step in range(1, rows_f)]
        c_peers = [lax.rem(c_place + step, count_c) for step in range(1, count_c)]
        greet([("fsdp", place) for place in f_peers] + [("ctx", place) for place in c_peers])
        order = c_peers + [c_place]
        copies_f = []
        for step, place in enumerate(f_peers):
            compute(place)
            row = []
            for index, part_place in enumerate(order):
                copy = push(
                    made.at[place, :, columns(part_place)],
                    landed.at[step, :, columns(part_place)],
                    send_f.at[step, index],
                    recv_f.at[step, index],
                    "fsdp",
                    place,
                )
                copy.start()
                row.append(copy)
            copies_f.append(row)
        compute(f_place)
        copies_c = []
        for index, part_place in enumerate(order):
            here = columns(part_place)
            value = made[f_place, :, here].astype(jnp.float32)
            for step in range(rows_f - 1):
                copies_f[step][index].wait_recv()
                value = value + landed[step, :, here].astype(jnp.float32)
            if index < count_c - 1:
                summed[index] = value.astype(jnp.bfloat16)
                copy = push(
                    summed.at[index],
                    landed_c.at[index],
                    send_c.at[index],
                    recv_c.at[index],
                    "ctx",
                    part_place,
                )
                copy.start()
                copies_c.append(copy)
            else:
                total[...] = value
        value = total[...]
        for index, copy in enumerate(copies_c):
            copy.wait_recv()
            value = value + landed_c[index].astype(jnp.float32)
        mine = columns(c_place)
        out[:, mine] = value.astype(jnp.bfloat16)
        copies_g = []
        for index, place in enumerate(c_peers):
            copy = push(
                out.at[:, mine],
                out.at[:, mine],
                send_g.at[index],
                recv_g.at[index],
                "ctx",
                place,
            )
            copy.start()
            copies_g.append(copy)
        for copy in copies_g:
            copy.wait()
        for copy in copies_c:
            copy.wait_send()
        for row in copies_f:
            for copy in row:
                copy.wait_send()


def padded_columns(array):
    return jnp.pad(array, ((0, 0), (0, padded(array.shape[1]) - array.shape[1])))


def reduce_grads(active, operands, collective_id):
    hid_in, d_qkv, att, d_mid, hid_mid, d_ff, act, grad_y, gain_in, gain_mid = operands
    rows_f = lax.axis_size("fsdp")
    count_c = lax.axis_size("ctx")
    tokens, features = hid_in.shape
    rows = features // rows_f
    assert att.shape == hid_in.shape

    def turned(array):
        return array.T.reshape(rows_f, rows, tokens)

    act_cols = act.shape[1] // rows_f
    act_blocks = act.reshape(tokens, rows_f, act_cols).transpose(1, 0, 2)
    gains = jnp.stack([gain_in, gain_mid], axis=-1).reshape(rows_f, rows, 2)
    gains = jnp.pad(gains, ((0, 0), (0, 0), (0, LANES - 2))).astype(jnp.bfloat16)
    d_mid = padded_columns(d_mid)
    d_qkv = padded_columns(d_qkv)
    off_ff = 0
    off_down = off_ff + d_ff.shape[1]
    off_gain = off_down + act.shape[1]
    off_out = off_gain + LANES
    off_qkv = off_out + d_mid.shape[1]
    end = off_qkv + d_qkv.shape[1]
    part = -(-end // (LANES * count_c)) * LANES
    whole = pl.BlockSpec(memory_space=pltpu.VMEM)
    out = pl.pallas_call(
        functools.partial(
            grads_kernel,
            active,
            rows_f,
            count_c,
            part,
            (off_ff, off_down, off_gain, off_out, off_qkv, end),
        ),
        out_shape=jax.ShapeDtypeStruct((rows, count_c * part), jnp.bfloat16),
        in_specs=[whole] * 9,
        out_specs=whole,
        scratch_shapes=[
            pltpu.VMEM((rows_f, rows, count_c * part), jnp.bfloat16),
            pltpu.VMEM((rows_f - 1, rows, count_c * part), jnp.bfloat16),
            pltpu.VMEM((count_c - 1, rows, part), jnp.bfloat16),
            pltpu.VMEM((count_c - 1, rows, part), jnp.bfloat16),
            pltpu.VMEM((rows, part), jnp.float32),
            pltpu.SemaphoreType.DMA((rows_f - 1, count_c)),
            pltpu.SemaphoreType.DMA((rows_f - 1, count_c)),
            pltpu.SemaphoreType.DMA((count_c - 1,)),
            pltpu.SemaphoreType.DMA((count_c - 1,)),
            pltpu.SemaphoreType.DMA((count_c - 1,)),
            pltpu.SemaphoreType.DMA((count_c - 1,)),
        ],
        compiler_params=call_options(collective_id),
        name="reduce_grads",
    )(
        turned(hid_in),
        turned(att),
        turned(hid_mid),
        turned(grad_y),
        d_qkv,
        d_mid,
        d_ff,
        act_blocks,
        gains,
    )
    return out, (off_ff, off_down, off_gain, off_out, off_qkv, act_cols)


def shifted(array, axis, by):
    devices = lax.axis_size(axis)
    pairs = [(i, i + by) for i in range(devices) if 0 <= i + by < devices]
    return lax.ppermute(array, axis, pairs)


def rope_tables(rope_rows):
    half_width = HEAD // 2
    frequency = THETA ** (-jnp.arange(half_width, dtype=jnp.float32) * (2.0 / HEAD))
    angle = rope_rows.astype(jnp.float32)[:, None] * frequency[None, :]
    return (jnp.cos(angle), jnp.sin(angle))


def rotate(vectors, cosine, sine):
    half_width = vectors.shape[-1] // 2
    front = vectors[..., :half_width]
    second = vectors[..., half_width:]
    cos_rows = cosine[:, None, :]
    sin_rows = sine[:, None, :]
    return jnp.concatenate(
        [front * cos_rows - second * sin_rows, second * cos_rows + front * sin_rows], axis=-1
    )


def normalize(field):
    factor = lax.rsqrt(jnp.mean(field * field, axis=-1, keepdims=True) + EPS)
    return (field * factor, factor)


def norm_back(grad_rows, normed, factor, gain):
    scaled = grad_rows * gain
    back = factor * (scaled - normed * jnp.mean(scaled * normed, axis=-1, keepdims=True))
    return (back, jnp.sum(grad_rows * normed, axis=0))


def block_size(row_count):
    return math.gcd(row_count, 512)


def positions_of(span_table, first_row, row_count, shard_rows):
    span_rows = shard_rows // 2
    slot_ids = jnp.arange(span_table.shape[0], dtype=jnp.int32)
    row_ids = first_row + jnp.arange(row_count, dtype=jnp.int32)
    slot_of = 2 * (row_ids // shard_rows) + row_ids % shard_rows // span_rows
    picked = jnp.sum(
        jnp.where(slot_of[:, None] == slot_ids[None, :], span_table[None, :], 0), axis=1
    )
    return picked * span_rows + row_ids % span_rows


def attend_forward(queries, gathered, span_table, local_pos, shard_rows):
    kv_width = gathered.shape[1] // 2
    score_scale = HEAD ** (-0.5)
    total_rows = gathered.shape[0]
    block_rows = block_size(total_rows)
    block_count = total_rows // block_rows
    key_pos = positions_of(span_table, 0, total_rows, shard_rows).reshape(block_count, block_rows)
    blocks = gathered.reshape(block_count, block_rows, gathered.shape[1])

    def masked_scores(kv_block, block_pos):
        key_heads = kv_block[:, :kv_width].reshape(block_rows, KV_HEADS, HEAD)
        scores = (
            jnp.einsum("rkgd,lkd->rkgl", queries, key_heads, preferred_element_type=jnp.float32)
            * score_scale
        )
        allowed = block_pos[None, :] <= local_pos[:, None]
        return jnp.where(allowed[:, None, None, :], scores, -math.inf)

    def total_pass(running, block_item):
        row_top, row_total = running
        scores = masked_scores(block_item[0], block_item[1])
        new_top = jnp.maximum(row_top, jnp.max(scores, axis=-1))
        anchor = jnp.where(new_top == -math.inf, 0.0, new_top)
        row_total = row_total * jnp.exp(row_top - anchor) + jnp.sum(
            jnp.exp(scores - anchor[..., None]), axis=-1
        )
        return ((new_top, row_total), None)

    initial = (
        jnp.full(queries.shape[:3], -math.inf, jnp.float32),
        jnp.zeros(queries.shape[:3], jnp.float32),
    )
    (row_top, row_total), unused = lax.scan(total_pass, initial, (blocks, key_pos))
    log_total = row_top + jnp.log(row_total)

    def value_pass(summed, block_item):
        kv_block, block_pos = block_item
        scores = masked_scores(kv_block, block_pos)
        value_heads = kv_block[:, kv_width:].reshape(block_rows, KV_HEADS, HEAD)
        probs = jnp.exp(scores - log_total[..., None]).astype(jnp.bfloat16)
        summed = summed + jnp.einsum(
            "rkgl,lkd->rkgd", probs, value_heads, preferred_element_type=jnp.float32
        )
        return (summed, None)

    summed, unused = lax.scan(value_pass, jnp.zeros(queries.shape, jnp.float32), (blocks, key_pos))
    return (summed.astype(jnp.bfloat16), log_total)


def attend_backward(
    queries, gathered, span_table, local_pos, log_total, grad_att, row_delta, shard_rows, call_id
):
    kv_width = gathered.shape[1] // 2
    score_scale = HEAD ** (-0.5)
    total_rows = gathered.shape[0]
    block_rows = block_size(total_rows)
    block_count = total_rows // block_rows
    key_pos = positions_of(span_table, 0, total_rows, shard_rows).reshape(block_count, block_rows)
    blocks = gathered.reshape(block_count, block_rows, gathered.shape[1])

    def backward_block(grad_q, block_item):
        kv_block, block_pos = block_item
        key_heads = kv_block[:, :kv_width].reshape(block_rows, KV_HEADS, HEAD)
        value_heads = kv_block[:, kv_width:].reshape(block_rows, KV_HEADS, HEAD)
        scores = (
            jnp.einsum("rkgd,lkd->rkgl", queries, key_heads, preferred_element_type=jnp.float32)
            * score_scale
        )
        allowed = block_pos[None, :] <= local_pos[:, None]
        scores = jnp.where(allowed[:, None, None, :], scores, -math.inf)
        probs = jnp.exp(scores - log_total[..., None])
        grad_v = jnp.einsum(
            "rkgl,rkgd->lkd",
            probs.astype(jnp.bfloat16),
            grad_att,
            preferred_element_type=jnp.float32,
        )
        grad_p = jnp.einsum(
            "rkgd,lkd->rkgl", grad_att, value_heads, preferred_element_type=jnp.float32
        )
        grad_s = (probs * (grad_p - row_delta[..., None])).astype(jnp.bfloat16)
        grad_q = (
            grad_q
            + jnp.einsum("rkgl,lkd->rkgd", grad_s, key_heads, preferred_element_type=jnp.float32)
            * score_scale
        )
        grad_k = (
            jnp.einsum("rkgl,rkgd->lkd", grad_s, queries, preferred_element_type=jnp.float32)
            * score_scale
        )
        joined = jnp.concatenate(
            [grad_k.reshape(block_rows, kv_width), grad_v.reshape(block_rows, kv_width)], axis=1
        )
        return (grad_q, joined)

    grad_q, pieces = lax.scan(
        backward_block, jnp.zeros(queries.shape, jnp.float32), (blocks, key_pos)
    )
    own_grads = collect(pieces.reshape(total_rows, 2 * kv_width), call_id)
    return (grad_q, own_grads)


def forward_layer(layer_input, rope_rows, params, span_table, local_pos, shard_rows, call_id):
    gain_in, w_q, w_k, w_v, w_o, gain_mid, w_g, w_u, w_d = params
    length = layer_input.shape[0]
    residual = layer_input.astype(jnp.float32)
    normed_in, scale_in = normalize(residual)
    hidden_in = (normed_in * gain_in).astype(jnp.bfloat16)
    cosine, sine = rope_tables(rope_rows)
    query = jnp.dot(hidden_in, w_q, preferred_element_type=jnp.float32).reshape(length, -1, HEAD)
    key_proj = jnp.dot(hidden_in, w_k, preferred_element_type=jnp.float32).reshape(
        length, KV_HEADS, HEAD
    )
    value = jnp.dot(hidden_in, w_v, preferred_element_type=jnp.float32).astype(jnp.bfloat16)
    query_b = rotate(query, cosine, sine).astype(jnp.bfloat16).reshape(length, KV_HEADS, -1, HEAD)
    key_b = rotate(key_proj, cosine, sine).astype(jnp.bfloat16).reshape(length, KV_HEADS * HEAD)
    kv_local = spread(jnp.concatenate([key_b, value], axis=1), call_id)
    attended, log_total = attend_forward(query_b, kv_local, span_table, local_pos, shard_rows)
    attended_flat = attended.reshape(length, -1)
    residual_mid = residual + jnp.dot(attended_flat, w_o, preferred_element_type=jnp.float32)
    normed_mid, scale_mid = normalize(residual_mid)
    hidden_mid = (normed_mid * gain_mid).astype(jnp.bfloat16)
    gate_pre = jnp.dot(hidden_mid, w_g, preferred_element_type=jnp.float32)
    up_pre = jnp.dot(hidden_mid, w_u, preferred_element_type=jnp.float32)
    active = (jax.nn.silu(gate_pre) * up_pre).astype(jnp.bfloat16)
    result = residual_mid + jnp.dot(active, w_d, preferred_element_type=jnp.float32)
    saved = (
        normed_in,
        scale_in,
        hidden_in,
        cosine,
        sine,
        query_b,
        kv_local,
        attended,
        log_total,
        normed_mid,
        scale_mid,
        hidden_mid,
        gate_pre,
        up_pre,
        active,
    )
    return (result, saved)


def backward_layer(saved, params, grad_y, span_table, local_pos, shard_rows, call_id):
    gain_in, w_q, w_k, w_v, w_o, gain_mid, w_g, w_u, w_d = params
    (
        normed_in,
        scale_in,
        hidden_in,
        cosine,
        sine,
        query_b,
        kv_local,
        attended,
        log_total,
        normed_mid,
        scale_mid,
        hidden_mid,
        gate_pre,
        up_pre,
        active,
    ) = saved
    length = grad_y.shape[0]
    grad_yb = grad_y.astype(jnp.bfloat16)
    grad_act = jnp.dot(grad_yb, w_d.T, preferred_element_type=jnp.float32)
    sigmoid_gate = jax.nn.sigmoid(gate_pre)
    grad_gate = (grad_act * up_pre * sigmoid_gate * (1.0 + gate_pre * (1.0 - sigmoid_gate))).astype(
        jnp.bfloat16
    )
    grad_up = (grad_act * gate_pre * sigmoid_gate).astype(jnp.bfloat16)
    grad_hmid = jnp.dot(grad_gate, w_g.T, preferred_element_type=jnp.float32) + jnp.dot(
        grad_up, w_u.T, preferred_element_type=jnp.float32
    )
    back_mid, grad_gmid = norm_back(grad_hmid, normed_mid, scale_mid, gain_mid)
    grad_mid = grad_y + back_mid
    grad_midb = grad_mid.astype(jnp.bfloat16)
    attended_flat = attended.reshape(length, -1)
    grad_att = (
        jnp.dot(grad_midb, w_o.T, preferred_element_type=jnp.float32)
        .astype(jnp.bfloat16)
        .reshape(attended.shape)
    )
    row_delta = jnp.sum(grad_att.astype(jnp.float32) * attended.astype(jnp.float32), axis=-1)
    grad_q, grad_kv = attend_backward(
        query_b, kv_local, span_table, local_pos, log_total, grad_att, row_delta, shard_rows, call_id
    )
    kv_width = kv_local.shape[1] // 2
    grad_qraw = (
        rotate(grad_q.reshape(length, -1, HEAD), cosine, -sine)
        .astype(jnp.bfloat16)
        .reshape(length, -1)
    )
    grad_kraw = (
        rotate(grad_kv[:, :kv_width].reshape(length, KV_HEADS, HEAD), cosine, -sine)
        .astype(jnp.bfloat16)
        .reshape(length, kv_width)
    )
    grad_vb = grad_kv[:, kv_width:].astype(jnp.bfloat16)
    grad_hin = (
        jnp.dot(grad_qraw, w_q.T, preferred_element_type=jnp.float32)
        + jnp.dot(grad_kraw, w_k.T, preferred_element_type=jnp.float32)
        + jnp.dot(grad_vb, w_v.T, preferred_element_type=jnp.float32)
    )
    back_in, grad_gin = norm_back(grad_hin, normed_in, scale_in, gain_in)
    grad_entry = grad_mid + back_in
    return (
        grad_entry,
        (
            hidden_in,
            jnp.concatenate([grad_qraw, grad_kraw, grad_vb], axis=1),
            attended_flat,
            grad_midb,
            hidden_mid,
            jnp.concatenate([grad_gate, grad_up], axis=1),
            active,
            grad_yb,
            grad_gin,
            grad_gmid,
        ),
    )


def body(
    block_input,
    cotangent,
    span_order,
    rope_ids,
    norm_in,
    w_query,
    w_key,
    w_value,
    w_out,
    norm_mid,
    w_gate,
    w_up,
    w_down,
):
    micro_count = block_input.shape[0]
    shard_rows = block_input.shape[2]
    ctx_place = lax.axis_index("ctx")
    leading = lax.axis_index("section") == 0
    local_pos = positions_of(span_order, ctx_place * shard_rows, shard_rows, shard_rows)
    gathered = (
        lax.all_gather(w_query[0], "fsdp", axis=0, tiled=True),
        lax.all_gather(w_key[0], "fsdp", axis=0, tiled=True),
        lax.all_gather(w_value[0], "fsdp", axis=0, tiled=True),
        lax.all_gather(w_out[0], "fsdp", axis=0, tiled=True),
        lax.all_gather(w_gate[0], "fsdp", axis=0, tiled=True),
        lax.all_gather(w_up[0], "fsdp", axis=0, tiled=True),
        lax.all_gather(w_down[0], "fsdp", axis=0, tiled=True),
    )
    params = (
        norm_in[0],
        gathered[0],
        gathered[1],
        gathered[2],
        gathered[3],
        norm_mid[0],
        gathered[4],
        gathered[5],
        gathered[6],
    )
    received = jnp.zeros(block_input.shape[2:], jnp.bfloat16)
    kept_states = []
    outputs = []
    for tick_index in range(micro_count + 1):
        fresh_rows = block_input[min(tick_index, micro_count - 1), 0]
        layer_input = jnp.where(leading, fresh_rows, received)
        rope_rows = jnp.where(
            leading,
            rope_ids[min(tick_index, micro_count - 1), 0],
            rope_ids[max(tick_index - 1, 0), 0],
        )
        result, saved = forward_layer(
            layer_input, rope_rows, params, span_order, local_pos, shard_rows, tick_index
        )
        sent_rows = result.astype(jnp.bfloat16)
        kept_states.append(saved)
        outputs.append(sent_rows)
        if tick_index < micro_count:
            received = shifted(sent_rows, "section", 1)
    returned = jnp.zeros(block_input.shape[2:], jnp.bfloat16)
    reduced = []
    grad_inputs = []
    for tick_index in range(micro_count + 1):
        if tick_index < micro_count:
            fresh_rows = cotangent[tick_index, 0]
        else:
            fresh_rows = jnp.zeros_like(cotangent[0, 0])
        arrival = jnp.where(leading, returned, fresh_rows).astype(jnp.float32)
        saved = jax.tree.map(
            lambda left, right: jnp.where(leading, left, right),
            kept_states[max(tick_index - 1, 0)],
            kept_states[min(tick_index + 1, micro_count)],
        )
        grad_entry, terms = backward_layer(
            saved, params, arrival, span_order, local_pos, shard_rows, 2 + tick_index
        )
        grad_inputs.append(grad_entry)
        if tick_index < micro_count:
            returned = shifted(grad_entry.astype(jnp.bfloat16), "section", -1)
        share, places = reduce_grads(1 - tick_index, terms, 4 + tick_index)
        reduced.append(share)
    layer_out = jnp.stack([jnp.where(leading, outputs[0], outputs[1])])
    grad_in = jnp.stack([jnp.where(leading, grad_inputs[1], grad_inputs[0])])
    layer_out = layer_out.reshape((1, micro_count, 1) + layer_out.shape[1:])
    grad_in = grad_in.reshape((1, micro_count, 1) + grad_in.shape[1:])
    share = jnp.where(leading, reduced[1], reduced[0]).astype(jnp.float32)
    off_ff, off_down, off_gain, off_out, off_qkv, act_cols = places

    def cut(first, width):
        return share[:, first : first + width]

    q_width, kv_width, ff_width = w_query.shape[2], w_key.shape[2], w_gate.shape[2]
    rows = share.shape[0]
    down_parts = block_input.shape[3] // rows
    grad_down = cut(off_down, down_parts * act_cols).reshape(rows, down_parts, act_cols)
    grad_down = grad_down.transpose(2, 1, 0).reshape(act_cols, down_parts * rows)
    totals = (
        cut(off_gain, 1)[:, 0],
        cut(off_qkv, q_width),
        cut(off_qkv + q_width, kv_width),
        cut(off_qkv + q_width + kv_width, kv_width),
        cut(off_out, block_input.shape[3]),
        cut(off_gain + 1, 1)[:, 0],
        cut(off_ff, ff_width),
        cut(off_ff + ff_width, ff_width),
        grad_down,
    )
    return (layer_out, grad_in) + tuple((summed_part[None] for summed_part in totals))


def solution(mesh):
    placed = (
        P(None, "fsdp", "ctx", None),
        P(None, "fsdp", "ctx", None),
        P(),
        P(None, "fsdp", "ctx"),
        P("section", None),
        P("section", "fsdp", None),
        P("section", "fsdp", None),
        P("section", "fsdp", None),
        P("section", "fsdp", None),
        P("section", None),
        P("section", "fsdp", None),
        P("section", "fsdp", None),
        P("section", "fsdp", None),
    )
    return jax.shard_map(
        body,
        mesh=mesh,
        in_specs=placed,
        out_specs=(
            P("section", None, "fsdp", "ctx", None),
            P("section", None, "fsdp", "ctx", None),
            P("section", "fsdp"),
            P("section", "fsdp", None),
            P("section", "fsdp", None),
            P("section", "fsdp", None),
            P("section", "fsdp", None),
            P("section", "fsdp"),
            P("section", "fsdp", None),
            P("section", "fsdp", None),
            P("section", "fsdp", None),
        ),
        check_vma=False,
    )
```

```python
import functools
import math

import jax
import jax.numpy as jnp
from jax import lax
from jax.experimental import pallas as pl
from jax.experimental.pallas import tpu as pltpu
from jax.sharding import PartitionSpec as P

KV_HEADS = 3
HEAD = 64


EPS = 1e-05
THETA = 100000.0


LANES = 128
VMEM_BYTES = 48 * 1024 * 1024


def padded(width):
    return -(-width // LANES) * LANES


def greet(peers):
    barrier = pltpu.get_barrier_semaphore()
    for axis, place in peers:
        pl.semaphore_signal(
            barrier, inc=1, device_id={axis: place}, device_id_type=pl.DeviceIdType.MESH
        )
    pl.semaphore_wait(barrier, len(peers))


def push(source, target, send_sem, recv_sem, axis, place):
    return pltpu.make_async_remote_copy(
        src_ref=source,
        dst_ref=target,
        send_sem=send_sem,
        recv_sem=recv_sem,
        device_id={axis: place},
        device_id_type=pl.DeviceIdType.MESH,
    )


def call_options(collective_id):
    return pltpu.CompilerParams(
        collective_id=collective_id, has_side_effects=True, vmem_limit_bytes=VMEM_BYTES
    )


def spread_kernel(count, own_ref, all_ref, send_sem, recv_sem):
    me = lax.axis_index("ctx")
    greet([("ctx", lax.rem(me + step, count)) for step in range(1, count)])
    copies = []
    for step in range(1, count):
        copy = push(
            own_ref,
            all_ref.at[me],
            send_sem.at[step - 1],
            recv_sem.at[step - 1],
            "ctx",
            lax.rem(me + step, count),
        )
        copy.start()
        copies.append(copy)
    all_ref[me] = own_ref[...]
    for copy in copies:
        copy.wait()


def spread(own, collective_id):
    count = lax.axis_size("ctx")
    whole = pl.BlockSpec(memory_space=pltpu.VMEM)
    return pl.pallas_call(
        functools.partial(spread_kernel, count),
        out_shape=jax.ShapeDtypeStruct((count,) + own.shape, own.dtype),
        in_specs=[whole],
        out_specs=whole,
        scratch_shapes=[
            pltpu.SemaphoreType.DMA((count - 1,)),
            pltpu.SemaphoreType.DMA((count - 1,)),
        ],
        compiler_params=call_options(collective_id),
        name="spread",
    )(own).reshape((count * own.shape[0],) + own.shape[1:])


def collect_kernel(count, pieces_ref, sum_ref, packed, landed, send_sem, recv_sem):
    me = lax.axis_index("ctx")
    greet([("ctx", lax.rem(me + step, count)) for step in range(1, count)])
    copies = []
    for step in range(1, count):
        place = lax.rem(me + step, count)
        packed[step - 1] = pieces_ref[place].astype(jnp.bfloat16)
        copy = push(
            packed.at[step - 1],
            landed.at[step - 1],
            send_sem.at[step - 1],
            recv_sem.at[step - 1],
            "ctx",
            place,
        )
        copy.start()
        copies.append(copy)
    total = pieces_ref[me]
    for step, copy in enumerate(copies):
        copy.wait_recv()
        total = total + landed[step].astype(jnp.float32)
    sum_ref[...] = total
    for copy in copies:
        copy.wait_send()


def collect(pieces, collective_id):
    count = lax.axis_size("ctx")
    whole = pl.BlockSpec(memory_space=pltpu.VMEM)
    blocks = pieces.reshape((count, -1) + pieces.shape[1:])
    slots = (count - 1,) + blocks.shape[1:]
    return pl.pallas_call(
        functools.partial(collect_kernel, count),
        out_shape=jax.ShapeDtypeStruct(blocks.shape[1:], jnp.float32),
        in_specs=[whole],
        out_specs=whole,
        scratch_shapes=[
            pltpu.VMEM(slots, jnp.bfloat16),
            pltpu.VMEM(slots, jnp.bfloat16),
            pltpu.SemaphoreType.DMA((count - 1,)),
            pltpu.SemaphoreType.DMA((count - 1,)),
        ],
        compiler_params=call_options(collective_id),
        name="collect",
    )(blocks)


def grads_kernel(
    active,
    rows_f,
    count_c,
    part,
    products,
    hid_in,
    att,
    hid_mid,
    grad_y,
    d_qkv,
    d_mid,
    d_ff,
    act,
    gains,
    out,
    made,
    landed,
    summed,
    landed_c,
    total,
    send_f,
    recv_f,
    send_c,
    recv_c,
    send_g,
    recv_g,
):
    off_ff, off_down, off_gain, off_out, off_qkv, end = products
    f_place = lax.axis_index("fsdp")
    c_place = lax.axis_index("ctx")

    def put(block, offset, left, right):
        width = right.shape[1]
        for first in range(0, width, 512):
            size = min(512, width - first)
            made[block, :, pl.ds(offset + first, size)] = jnp.dot(
                left, right[:, first : first + size], preferred_element_type=jnp.float32
            ).astype(jnp.bfloat16)

    def compute(block):
        put(block, off_ff, hid_mid[block], d_ff[...])
        step_rows = act.shape[2]
        for index in range(rows_f):
            put(block, off_down + index * step_rows, grad_y[index], act[block])
        made[block, :, pl.ds(off_gain, LANES)] = gains[block]
        put(block, off_out, att[block], d_mid[...])
        put(block, off_qkv, hid_in[block], d_qkv[...])
        if end < count_c * part:
            made[block, :, pl.ds(end, count_c * part - end)] = jnp.zeros(
                (made.shape[1], count_c * part - end), jnp.bfloat16
            )

    def columns(index):
        return pl.ds(pl.multiple_of(index * part, LANES), part)

    @pl.when(lax.axis_index("section") == active)
    def run():
        f_peers = [lax.rem(f_place + step, rows_f) for step in range(1, rows_f)]
        c_peers = [lax.rem(c_place + step, count_c) for step in range(1, count_c)]
        greet([("fsdp", place) for place in f_peers] + [("ctx", place) for place in c_peers])
        order = c_peers + [c_place]
        copies_f = [[] for place in f_peers]

        def send_part(step, index):
            here = columns(order[index])
            copy = push(
                made.at[f_peers[step], :, here],
                landed.at[step, :, here],
                send_f.at[step, index],
                recv_f.at[step, index],
                "fsdp",
                f_peers[step],
            )
            copy.start()
            copies_f[step].append(copy)

        for step, place in enumerate(f_peers):
            compute(place)
            send_part(step, 0)
        for index in range(1, count_c):
            for step in range(rows_f - 1):
                send_part(step, index)
        compute(f_place)
        copies_c = []
        for index, part_place in enumerate(order):
            here = columns(part_place)
            value = made[f_place, :, here].astype(jnp.float32)
            for step in range(rows_f - 1):
                copies_f[step][index].wait_recv()
                value = value + landed[step, :, here].astype(jnp.float32)
            if index < count_c - 1:
                summed[index] = value.astype(jnp.bfloat16)
                copy = push(
                    summed.at[index],
                    landed_c.at[index],
                    send_c.at[index],
                    recv_c.at[index],
                    "ctx",
                    part_place,
                )
                copy.start()
                copies_c.append(copy)
            else:
                total[...] = value
        value = total[...]
        for index, copy in enumerate(copies_c):
            copy.wait_recv()
            value = value + landed_c[index].astype(jnp.float32)
        mine = columns(c_place)
        out[:, mine] = value.astype(jnp.bfloat16)
        copies_g = []
        for index, place in enumerate(c_peers):
            copy = push(
                out.at[:, mine],
                out.at[:, mine],
                send_g.at[index],
                recv_g.at[index],
                "ctx",
                place,
            )
            copy.start()
            copies_g.append(copy)
        for copy in copies_g:
            copy.wait()
        for copy in copies_c:
            copy.wait_send()
        for row in copies_f:
            for copy in row:
                copy.wait_send()


def padded_columns(array):
    return jnp.pad(array, ((0, 0), (0, padded(array.shape[1]) - array.shape[1])))


def reduce_grads(active, operands, collective_id):
    hid_in, d_qkv, att, d_mid, hid_mid, d_ff, act, grad_y, gain_in, gain_mid = operands
    rows_f = lax.axis_size("fsdp")
    count_c = lax.axis_size("ctx")
    tokens, features = hid_in.shape
    rows = features // rows_f
    assert att.shape == hid_in.shape

    def turned(array):
        return array.T.reshape(rows_f, rows, tokens)

    act_cols = act.shape[1] // rows_f
    act_blocks = act.reshape(tokens, rows_f, act_cols).transpose(1, 0, 2)
    gains = jnp.stack([gain_in, gain_mid], axis=-1).reshape(rows_f, rows, 2)
    gains = jnp.pad(gains, ((0, 0), (0, 0), (0, LANES - 2))).astype(jnp.bfloat16)
    d_mid = padded_columns(d_mid)
    d_qkv = padded_columns(d_qkv)
    off_ff = 0
    off_down = off_ff + d_ff.shape[1]
    off_gain = off_down + act.shape[1]
    off_out = off_gain + LANES
    off_qkv = off_out + d_mid.shape[1]
    end = off_qkv + d_qkv.shape[1]
    part = -(-end // (LANES * count_c)) * LANES
    whole = pl.BlockSpec(memory_space=pltpu.VMEM)
    out = pl.pallas_call(
        functools.partial(
            grads_kernel,
            active,
            rows_f,
            count_c,
            part,
            (off_ff, off_down, off_gain, off_out, off_qkv, end),
        ),
        out_shape=jax.ShapeDtypeStruct((rows, count_c * part), jnp.bfloat16),
        in_specs=[whole] * 9,
        out_specs=whole,
        scratch_shapes=[
            pltpu.VMEM((rows_f, rows, count_c * part), jnp.bfloat16),
            pltpu.VMEM((rows_f - 1, rows, count_c * part), jnp.bfloat16),
            pltpu.VMEM((count_c - 1, rows, part), jnp.bfloat16),
            pltpu.VMEM((count_c - 1, rows, part), jnp.bfloat16),
            pltpu.VMEM((rows, part), jnp.float32),
            pltpu.SemaphoreType.DMA((rows_f - 1, count_c)),
            pltpu.SemaphoreType.DMA((rows_f - 1, count_c)),
            pltpu.SemaphoreType.DMA((count_c - 1,)),
            pltpu.SemaphoreType.DMA((count_c - 1,)),
            pltpu.SemaphoreType.DMA((count_c - 1,)),
            pltpu.SemaphoreType.DMA((count_c - 1,)),
        ],
        compiler_params=call_options(collective_id),
        name="reduce_grads",
    )(
        turned(hid_in),
        turned(att),
        turned(hid_mid),
        turned(grad_y),
        d_qkv,
        d_mid,
        d_ff,
        act_blocks,
        gains,
    )
    return out, (off_ff, off_down, off_gain, off_out, off_qkv, act_cols)


def weights_kernel(active, number, held, *refs):
    shards = refs[:number]
    outs = refs[number * (2 if held else 1) :][:number]
    send_sem, recv_sem, own_sem = refs[-3:]
    me = lax.axis_index("fsdp")
    near = me + 1 - 2 * lax.rem(me, 2)
    far = lax.rem(me + 2, 4)

    @pl.when(lax.axis_index("section") == active)
    def run():
        greet([("fsdp", near), ("fsdp", far)])

        def halves(index):
            rows = shards[index].shape[0]
            first = rows // 2 // 16 * 16
            return pl.ds(0, first), pl.ds(first, rows - first)

        def send(index, slot, source, block, rows, place):
            copy = push(
                source,
                outs[index].at[block, rows],
                send_sem.at[index, slot],
                recv_sem.at[index, slot],
                "fsdp",
                place,
            )
            copy.start()
            return copy

        copies = []
        for index in range(number):
            top, low = halves(index)
            copies.append(
                [
                    send(index, 0, shards[index].at[top], me, top, near),
                    send(index, 1, shards[index].at[low], me, low, far),
                    send(index, 2, shards[index].at[low], me, low, near),
                    send(index, 3, shards[index].at[top], me, top, far),
                ]
            )
        locals_ = []
        for index in range(number):
            copy = pltpu.make_async_copy(shards[index], outs[index].at[me], own_sem.at[index])
            copy.start()
            locals_.append(copy)
        for index in range(number):
            top, low = halves(index)
            copies[index][0].wait_recv()
            copies[index].append(send(index, 4, outs[index].at[near, top], near, top, far))
            copies[index][1].wait_recv()
            copies[index].append(send(index, 5, outs[index].at[far, low], far, low, near))
        for index in range(number):
            for slot in range(2, 6):
                copies[index][slot].wait_recv()
            for copy in copies[index]:
                copy.wait_send()
            locals_[index].wait()


def gather_weights(active, shards, held, collective_id):
    count = lax.axis_size("fsdp")
    assert count == 4
    number = len(shards)
    anywhere = pl.BlockSpec(memory_space=pl.ANY)
    operands = tuple(shards) + tuple(held or ())
    return pl.pallas_call(
        functools.partial(weights_kernel, active, number, held is not None),
        out_shape=[jax.ShapeDtypeStruct((count,) + shard.shape, shard.dtype) for shard in shards],
        in_specs=[anywhere] * len(operands),
        out_specs=[anywhere] * number,
        scratch_shapes=[
            pltpu.SemaphoreType.DMA((number, 6)),
            pltpu.SemaphoreType.DMA((number, 6)),
            pltpu.SemaphoreType.DMA((number,)),
        ],
        input_output_aliases={number + index: index for index in range(len(held or ()))},
        compiler_params=call_options(collective_id),
        name="gather_weights",
    )(*operands)


def shifted(array, axis, by):
    devices = lax.axis_size(axis)
    pairs = [(i, i + by) for i in range(devices) if 0 <= i + by < devices]
    return lax.ppermute(array, axis, pairs)


def rope_tables(rope_rows):
    half_width = HEAD // 2
    frequency = THETA ** (-jnp.arange(half_width, dtype=jnp.float32) * (2.0 / HEAD))
    angle = rope_rows.astype(jnp.float32)[:, None] * frequency[None, :]
    return (jnp.cos(angle), jnp.sin(angle))


def rotate(vectors, cosine, sine):
    half_width = vectors.shape[-1] // 2
    front = vectors[..., :half_width]
    second = vectors[..., half_width:]
    cos_rows = cosine[:, None, :]
    sin_rows = sine[:, None, :]
    return jnp.concatenate(
        [front * cos_rows - second * sin_rows, second * cos_rows + front * sin_rows], axis=-1
    )


def normalize(field):
    factor = lax.rsqrt(jnp.mean(field * field, axis=-1, keepdims=True) + EPS)
    return (field * factor, factor)


def norm_back(grad_rows, normed, factor, gain):
    scaled = grad_rows * gain
    back = factor * (scaled - normed * jnp.mean(scaled * normed, axis=-1, keepdims=True))
    return (back, jnp.sum(grad_rows * normed, axis=0))


def block_size(row_count):
    return math.gcd(row_count, 512)


def positions_of(span_table, first_row, row_count, shard_rows):
    span_rows = shard_rows // 2
    slot_ids = jnp.arange(span_table.shape[0], dtype=jnp.int32)
    row_ids = first_row + jnp.arange(row_count, dtype=jnp.int32)
    slot_of = 2 * (row_ids // shard_rows) + row_ids % shard_rows // span_rows
    picked = jnp.sum(
        jnp.where(slot_of[:, None] == slot_ids[None, :], span_table[None, :], 0), axis=1
    )
    return picked * span_rows + row_ids % span_rows


def attend_forward(queries, gathered, span_table, local_pos, shard_rows):
    kv_width = gathered.shape[1] // 2
    score_scale = HEAD ** (-0.5)
    total_rows = gathered.shape[0]
    block_rows = block_size(total_rows)
    block_count = total_rows // block_rows
    key_pos = positions_of(span_table, 0, total_rows, shard_rows).reshape(block_count, block_rows)
    blocks = gathered.reshape(block_count, block_rows, gathered.shape[1])

    def masked_scores(kv_block, block_pos):
        key_heads = kv_block[:, :kv_width].reshape(block_rows, KV_HEADS, HEAD)
        scores = (
            jnp.einsum("rkgd,lkd->rkgl", queries, key_heads, preferred_element_type=jnp.float32)
            * score_scale
        )
        allowed = block_pos[None, :] <= local_pos[:, None]
        return jnp.where(allowed[:, None, None, :], scores, -math.inf)

    def total_pass(running, block_item):
        row_top, row_total = running
        scores = masked_scores(block_item[0], block_item[1])
        new_top = jnp.maximum(row_top, jnp.max(scores, axis=-1))
        anchor = jnp.where(new_top == -math.inf, 0.0, new_top)
        row_total = row_total * jnp.exp(row_top - anchor) + jnp.sum(
            jnp.exp(scores - anchor[..., None]), axis=-1
        )
        return ((new_top, row_total), None)

    initial = (
        jnp.full(queries.shape[:3], -math.inf, jnp.float32),
        jnp.zeros(queries.shape[:3], jnp.float32),
    )
    (row_top, row_total), unused = lax.scan(total_pass, initial, (blocks, key_pos))
    log_total = row_top + jnp.log(row_total)

    def value_pass(summed, block_item):
        kv_block, block_pos = block_item
        scores = masked_scores(kv_block, block_pos)
        value_heads = kv_block[:, kv_width:].reshape(block_rows, KV_HEADS, HEAD)
        probs = jnp.exp(scores - log_total[..., None]).astype(jnp.bfloat16)
        summed = summed + jnp.einsum(
            "rkgl,lkd->rkgd", probs, value_heads, preferred_element_type=jnp.float32
        )
        return (summed, None)

    summed, unused = lax.scan(value_pass, jnp.zeros(queries.shape, jnp.float32), (blocks, key_pos))
    return (summed.astype(jnp.bfloat16), log_total)


def attend_backward(
    queries, gathered, span_table, local_pos, log_total, grad_att, row_delta, shard_rows, call_id
):
    kv_width = gathered.shape[1] // 2
    score_scale = HEAD ** (-0.5)
    total_rows = gathered.shape[0]
    block_rows = block_size(total_rows)
    block_count = total_rows // block_rows
    key_pos = positions_of(span_table, 0, total_rows, shard_rows).reshape(block_count, block_rows)
    blocks = gathered.reshape(block_count, block_rows, gathered.shape[1])

    def backward_block(grad_q, block_item):
        kv_block, block_pos = block_item
        key_heads = kv_block[:, :kv_width].reshape(block_rows, KV_HEADS, HEAD)
        value_heads = kv_block[:, kv_width:].reshape(block_rows, KV_HEADS, HEAD)
        scores = (
            jnp.einsum("rkgd,lkd->rkgl", queries, key_heads, preferred_element_type=jnp.float32)
            * score_scale
        )
        allowed = block_pos[None, :] <= local_pos[:, None]
        scores = jnp.where(allowed[:, None, None, :], scores, -math.inf)
        probs = jnp.exp(scores - log_total[..., None])
        grad_v = jnp.einsum(
            "rkgl,rkgd->lkd",
            probs.astype(jnp.bfloat16),
            grad_att,
            preferred_element_type=jnp.float32,
        )
        grad_p = jnp.einsum(
            "rkgd,lkd->rkgl", grad_att, value_heads, preferred_element_type=jnp.float32
        )
        grad_s = (probs * (grad_p - row_delta[..., None])).astype(jnp.bfloat16)
        grad_q = (
            grad_q
            + jnp.einsum("rkgl,lkd->rkgd", grad_s, key_heads, preferred_element_type=jnp.float32)
            * score_scale
        )
        grad_k = (
            jnp.einsum("rkgl,rkgd->lkd", grad_s, queries, preferred_element_type=jnp.float32)
            * score_scale
        )
        joined = jnp.concatenate(
            [grad_k.reshape(block_rows, kv_width), grad_v.reshape(block_rows, kv_width)], axis=1
        )
        return (grad_q, joined)

    grad_q, pieces = lax.scan(
        backward_block, jnp.zeros(queries.shape, jnp.float32), (blocks, key_pos)
    )
    own_grads = collect(pieces.reshape(total_rows, 2 * kv_width), call_id)
    return (grad_q, own_grads)


def forward_layer(layer_input, rope_rows, params, span_table, local_pos, shard_rows, call_id):
    gain_in, w_q, w_k, w_v, w_o, gain_mid, w_g, w_u, w_d = params
    length = layer_input.shape[0]
    residual = layer_input.astype(jnp.float32)
    normed_in, scale_in = normalize(residual)
    hidden_in = (normed_in * gain_in).astype(jnp.bfloat16)
    cosine, sine = rope_tables(rope_rows)
    query = jnp.dot(hidden_in, w_q, preferred_element_type=jnp.float32).reshape(length, -1, HEAD)
    key_proj = jnp.dot(hidden_in, w_k, preferred_element_type=jnp.float32).reshape(
        length, KV_HEADS, HEAD
    )
    value = jnp.dot(hidden_in, w_v, preferred_element_type=jnp.float32).astype(jnp.bfloat16)
    query_b = rotate(query, cosine, sine).astype(jnp.bfloat16).reshape(length, KV_HEADS, -1, HEAD)
    key_b = rotate(key_proj, cosine, sine).astype(jnp.bfloat16).reshape(length, KV_HEADS * HEAD)
    kv_local = spread(jnp.concatenate([key_b, value], axis=1), call_id)
    attended, log_total = attend_forward(query_b, kv_local, span_table, local_pos, shard_rows)
    attended_flat = attended.reshape(length, -1)
    residual_mid = residual + jnp.dot(attended_flat, w_o, preferred_element_type=jnp.float32)
    normed_mid, scale_mid = normalize(residual_mid)
    hidden_mid = (normed_mid * gain_mid).astype(jnp.bfloat16)
    gate_pre = jnp.dot(hidden_mid, w_g, preferred_element_type=jnp.float32)
    up_pre = jnp.dot(hidden_mid, w_u, preferred_element_type=jnp.float32)
    active = (jax.nn.silu(gate_pre) * up_pre).astype(jnp.bfloat16)
    result = residual_mid + jnp.dot(active, w_d, preferred_element_type=jnp.float32)
    saved = (
        normed_in,
        scale_in,
        hidden_in,
        cosine,
        sine,
        query_b,
        kv_local,
        attended,
        log_total,
        normed_mid,
        scale_mid,
        hidden_mid,
        gate_pre,
        up_pre,
        active,
    )
    return (result, saved)


def backward_layer(saved, params, grad_y, span_table, local_pos, shard_rows, call_id):
    gain_in, w_q, w_k, w_v, w_o, gain_mid, w_g, w_u, w_d = params
    (
        normed_in,
        scale_in,
        hidden_in,
        cosine,
        sine,
        query_b,
        kv_local,
        attended,
        log_total,
        normed_mid,
        scale_mid,
        hidden_mid,
        gate_pre,
        up_pre,
        active,
    ) = saved
    length = grad_y.shape[0]
    grad_yb = grad_y.astype(jnp.bfloat16)
    grad_act = jnp.dot(grad_yb, w_d.T, preferred_element_type=jnp.float32)
    sigmoid_gate = jax.nn.sigmoid(gate_pre)
    grad_gate = (grad_act * up_pre * sigmoid_gate * (1.0 + gate_pre * (1.0 - sigmoid_gate))).astype(
        jnp.bfloat16
    )
    grad_up = (grad_act * gate_pre * sigmoid_gate).astype(jnp.bfloat16)
    grad_hmid = jnp.dot(grad_gate, w_g.T, preferred_element_type=jnp.float32) + jnp.dot(
        grad_up, w_u.T, preferred_element_type=jnp.float32
    )
    back_mid, grad_gmid = norm_back(grad_hmid, normed_mid, scale_mid, gain_mid)
    grad_mid = grad_y + back_mid
    grad_midb = grad_mid.astype(jnp.bfloat16)
    attended_flat = attended.reshape(length, -1)
    grad_att = (
        jnp.dot(grad_midb, w_o.T, preferred_element_type=jnp.float32)
        .astype(jnp.bfloat16)
        .reshape(attended.shape)
    )
    row_delta = jnp.sum(grad_att.astype(jnp.float32) * attended.astype(jnp.float32), axis=-1)
    grad_q, grad_kv = attend_backward(
        query_b, kv_local, span_table, local_pos, log_total, grad_att, row_delta, shard_rows, call_id
    )
    kv_width = kv_local.shape[1] // 2
    grad_qraw = (
        rotate(grad_q.reshape(length, -1, HEAD), cosine, -sine)
        .astype(jnp.bfloat16)
        .reshape(length, -1)
    )
    grad_kraw = (
        rotate(grad_kv[:, :kv_width].reshape(length, KV_HEADS, HEAD), cosine, -sine)
        .astype(jnp.bfloat16)
        .reshape(length, kv_width)
    )
    grad_vb = grad_kv[:, kv_width:].astype(jnp.bfloat16)
    grad_hin = (
        jnp.dot(grad_qraw, w_q.T, preferred_element_type=jnp.float32)
        + jnp.dot(grad_kraw, w_k.T, preferred_element_type=jnp.float32)
        + jnp.dot(grad_vb, w_v.T, preferred_element_type=jnp.float32)
    )
    back_in, grad_gin = norm_back(grad_hin, normed_in, scale_in, gain_in)
    grad_entry = grad_mid + back_in
    return (
        grad_entry,
        (
            hidden_in,
            jnp.concatenate([grad_qraw, grad_kraw, grad_vb], axis=1),
            attended_flat,
            grad_midb,
            hidden_mid,
            jnp.concatenate([grad_gate, grad_up], axis=1),
            active,
            grad_yb,
            grad_gin,
            grad_gmid,
        ),
    )


def body(
    block_input,
    cotangent,
    span_order,
    rope_ids,
    norm_in,
    w_query,
    w_key,
    w_value,
    w_out,
    norm_mid,
    w_gate,
    w_up,
    w_down,
):
    micro_count = block_input.shape[0]
    shard_rows = block_input.shape[2]
    ctx_place = lax.axis_index("ctx")
    leading = lax.axis_index("section") == 0
    local_pos = positions_of(span_order, ctx_place * shard_rows, shard_rows, shard_rows)
    shards = (w_query[0], w_key[0], w_value[0], w_out[0], w_gate[0], w_up[0], w_down[0])
    held = gather_weights(0, shards, None, 6)

    def params_of(blocks):
        full = [block.reshape((-1, block.shape[2])) for block in blocks]
        return (norm_in[0], *full[:4], norm_mid[0], *full[4:])

    params = params_of(held)
    received = jnp.zeros(block_input.shape[2:], jnp.bfloat16)
    kept_states = []
    outputs = []
    for tick_index in range(micro_count + 1):
        fresh_rows = block_input[min(tick_index, micro_count - 1), 0]
        layer_input = jnp.where(leading, fresh_rows, received)
        rope_rows = jnp.where(
            leading,
            rope_ids[min(tick_index, micro_count - 1), 0],
            rope_ids[max(tick_index - 1, 0), 0],
        )
        result, saved = forward_layer(
            layer_input, rope_rows, params, span_order, local_pos, shard_rows, tick_index
        )
        sent_rows = result.astype(jnp.bfloat16)
        kept_states.append(saved)
        outputs.append(sent_rows)
        if tick_index < micro_count:
            sent_rows, held = lax.optimization_barrier((sent_rows, tuple(held)))
            held = gather_weights(1, shards, held, 7)
            sent_rows, held = lax.optimization_barrier((sent_rows, tuple(held)))
            params = params_of(held)
            received = shifted(sent_rows, "section", 1)
    returned = jnp.zeros(block_input.shape[2:], jnp.bfloat16)
    reduced = []
    grad_inputs = []
    for tick_index in range(micro_count + 1):
        if tick_index < micro_count:
            fresh_rows = cotangent[tick_index, 0]
        else:
            fresh_rows = jnp.zeros_like(cotangent[0, 0])
        arrival = jnp.where(leading, returned, fresh_rows).astype(jnp.float32)
        saved = jax.tree.map(
            lambda left, right: jnp.where(leading, left, right),
            kept_states[max(tick_index - 1, 0)],
            kept_states[min(tick_index + 1, micro_count)],
        )
        grad_entry, terms = backward_layer(
            saved, params, arrival, span_order, local_pos, shard_rows, 2 + tick_index
        )
        grad_inputs.append(grad_entry)
        if tick_index < micro_count:
            returned = shifted(grad_entry.astype(jnp.bfloat16), "section", -1)
        share, places = reduce_grads(1 - tick_index, terms, 4 + tick_index)
        reduced.append(share)
    layer_out = jnp.stack([jnp.where(leading, outputs[0], outputs[1])])
    grad_in = jnp.stack([jnp.where(leading, grad_inputs[1], grad_inputs[0])])
    layer_out = layer_out.reshape((1, micro_count, 1) + layer_out.shape[1:])
    grad_in = grad_in.reshape((1, micro_count, 1) + grad_in.shape[1:])
    share = jnp.where(leading, reduced[1], reduced[0]).astype(jnp.float32)
    off_ff, off_down, off_gain, off_out, off_qkv, act_cols = places

    def cut(first, width):
        return share[:, first : first + width]

    q_width, kv_width, ff_width = w_query.shape[2], w_key.shape[2], w_gate.shape[2]
    rows = share.shape[0]
    down_parts = block_input.shape[3] // rows
    grad_down = cut(off_down, down_parts * act_cols).reshape(rows, down_parts, act_cols)
    grad_down = grad_down.transpose(2, 1, 0).reshape(act_cols, down_parts * rows)
    totals = (
        cut(off_gain, 1)[:, 0],
        cut(off_qkv, q_width),
        cut(off_qkv + q_width, kv_width),
        cut(off_qkv + q_width + kv_width, kv_width),
        cut(off_out, block_input.shape[3]),
        cut(off_gain + 1, 1)[:, 0],
        cut(off_ff, ff_width),
        cut(off_ff + ff_width, ff_width),
        grad_down,
    )
    return (layer_out, grad_in) + tuple((summed_part[None] for summed_part in totals))


def solution(mesh):
    placed = (
        P(None, "fsdp", "ctx", None),
        P(None, "fsdp", "ctx", None),
        P(),
        P(None, "fsdp", "ctx"),
        P("section", None),
        P("section", "fsdp", None),
        P("section", "fsdp", None),
        P("section", "fsdp", None),
        P("section", "fsdp", None),
        P("section", None),
        P("section", "fsdp", None),
        P("section", "fsdp", None),
        P("section", "fsdp", None),
    )
    return jax.shard_map(
        body,
        mesh=mesh,
        in_specs=placed,
        out_specs=(
            P("section", None, "fsdp", "ctx", None),
            P("section", None, "fsdp", "ctx", None),
            P("section", "fsdp"),
            P("section", "fsdp", None),
            P("section", "fsdp", None),
            P("section", "fsdp", None),
            P("section", "fsdp", None),
            P("section", "fsdp"),
            P("section", "fsdp", None),
            P("section", "fsdp", None),
            P("section", "fsdp", None),
        ),
        check_vma=False,
    )
```

```python
import functools
import math

import jax
import jax.numpy as jnp
from jax import lax
from jax.experimental import pallas as pl
from jax.experimental.pallas import tpu as pltpu
from jax.sharding import PartitionSpec as P

KV_HEADS = 3
HEAD = 64


EPS = 1e-05
THETA = 100000.0


LANES = 128
VMEM_BYTES = 48 * 1024 * 1024


def padded(width):
    return -(-width // LANES) * LANES


def greet(peers):
    barrier = pltpu.get_barrier_semaphore()
    for axis, place in peers:
        pl.semaphore_signal(
            barrier, inc=1, device_id={axis: place}, device_id_type=pl.DeviceIdType.MESH
        )
    pl.semaphore_wait(barrier, len(peers))


def push(source, target, send_sem, recv_sem, axis, place):
    return pltpu.make_async_remote_copy(
        src_ref=source,
        dst_ref=target,
        send_sem=send_sem,
        recv_sem=recv_sem,
        device_id={axis: place},
        device_id_type=pl.DeviceIdType.MESH,
    )


def call_options(collective_id):
    return pltpu.CompilerParams(
        collective_id=collective_id, has_side_effects=True, vmem_limit_bytes=VMEM_BYTES
    )


def spread_kernel(count, own_ref, all_ref, send_sem, recv_sem):
    me = lax.axis_index("ctx")
    greet([("ctx", lax.rem(me + step, count)) for step in range(1, count)])
    copies = []
    for step in range(1, count):
        copy = push(
            own_ref,
            all_ref.at[me],
            send_sem.at[step - 1],
            recv_sem.at[step - 1],
            "ctx",
            lax.rem(me + step, count),
        )
        copy.start()
        copies.append(copy)
    all_ref[me] = own_ref[...]
    for copy in copies:
        copy.wait()


def spread(own, collective_id):
    count = lax.axis_size("ctx")
    whole = pl.BlockSpec(memory_space=pltpu.VMEM)
    return pl.pallas_call(
        functools.partial(spread_kernel, count),
        out_shape=jax.ShapeDtypeStruct((count,) + own.shape, own.dtype),
        in_specs=[whole],
        out_specs=whole,
        scratch_shapes=[
            pltpu.SemaphoreType.DMA((count - 1,)),
            pltpu.SemaphoreType.DMA((count - 1,)),
        ],
        compiler_params=call_options(collective_id),
        name="spread",
    )(own).reshape((count * own.shape[0],) + own.shape[1:])


def collect_kernel(count, pieces_ref, sum_ref, packed, landed, send_sem, recv_sem):
    me = lax.axis_index("ctx")
    greet([("ctx", lax.rem(me + step, count)) for step in range(1, count)])
    copies = []
    for step in range(1, count):
        place = lax.rem(me + step, count)
        packed[step - 1] = pieces_ref[place].astype(jnp.bfloat16)
        copy = push(
            packed.at[step - 1],
            landed.at[step - 1],
            send_sem.at[step - 1],
            recv_sem.at[step - 1],
            "ctx",
            place,
        )
        copy.start()
        copies.append(copy)
    total = pieces_ref[me]
    for step, copy in enumerate(copies):
        copy.wait_recv()
        total = total + landed[step].astype(jnp.float32)
    sum_ref[...] = total
    for copy in copies:
        copy.wait_send()


def collect(pieces, collective_id):
    count = lax.axis_size("ctx")
    whole = pl.BlockSpec(memory_space=pltpu.VMEM)
    blocks = pieces.reshape((count, -1) + pieces.shape[1:])
    slots = (count - 1,) + blocks.shape[1:]
    return pl.pallas_call(
        functools.partial(collect_kernel, count),
        out_shape=jax.ShapeDtypeStruct(blocks.shape[1:], jnp.float32),
        in_specs=[whole],
        out_specs=whole,
        scratch_shapes=[
            pltpu.VMEM(slots, jnp.bfloat16),
            pltpu.VMEM(slots, jnp.bfloat16),
            pltpu.SemaphoreType.DMA((count - 1,)),
            pltpu.SemaphoreType.DMA((count - 1,)),
        ],
        compiler_params=call_options(collective_id),
        name="collect",
    )(blocks)


def grads_kernel(
    active,
    rows_f,
    count_c,
    part,
    products,
    hid_in,
    att,
    hid_mid,
    grad_y,
    d_q,
    d_k,
    d_v,
    d_mid,
    d_gate,
    d_up,
    act,
    in_terms,
    mid_terms,
    out,
    made,
    landed,
    summed,
    landed_c,
    total,
    send_f,
    recv_f,
    send_c,
    recv_c,
    send_g,
    recv_g,
):
    offsets, end = products
    f_place = lax.axis_index("fsdp")
    c_place = lax.axis_index("ctx")
    rows = made.shape[1]

    def across(left, right):
        return lax.dot_general(
            left, right, (((0,), (0,)), ((), ())), preferred_element_type=jnp.float32
        ).astype(jnp.bfloat16)

    def put(offset, left, right):
        width = right.shape[1]
        tail = padded(width) - width
        if tail:
            for block in range(rows_f):
                made[block, :, pl.ds(offset + width, tail)] = jnp.zeros((rows, tail), made.dtype)
        for first in range(0, width, 512):
            size = min(512, width - first)
            product = across(left[...], right[:, first : first + size])
            for block in range(rows_f):
                made[block, :, pl.ds(offset + first, size)] = product[
                    block * rows : (block + 1) * rows
                ]

    def compute():
        put(offsets[0], hid_mid, d_gate)
        put(offsets[1], hid_mid, d_up)
        width = act.shape[1] // rows_f
        for block in range(rows_f):
            product = across(grad_y[...], act[:, block * width : (block + 1) * width])
            for index in range(rows_f):
                made[block, :, pl.ds(offsets[2] + index * width, width)] = product[
                    index * rows : (index + 1) * rows
                ]
        ones = jnp.ones((act.shape[0], LANES), jnp.bfloat16)
        put(offsets[3], in_terms, ones)
        put(offsets[4], mid_terms, ones)
        put(offsets[5], att, d_mid)
        put(offsets[6], hid_in, d_q)
        put(offsets[7], hid_in, d_k)
        put(offsets[8], hid_in, d_v)
        rest = count_c * part - end
        if rest:
            for block in range(rows_f):
                made[block, :, pl.ds(end, rest)] = jnp.zeros((rows, rest), made.dtype)

    def columns(index):
        return pl.ds(pl.multiple_of(index * part, LANES), part)

    @pl.when(lax.axis_index("section") == active)
    def run():
        f_peers = [lax.rem(f_place + step, rows_f) for step in range(1, rows_f)]
        c_peers = [lax.rem(c_place + step, count_c) for step in range(1, count_c)]
        greet([("fsdp", place) for place in f_peers] + [("ctx", place) for place in c_peers])
        order = c_peers + [c_place]
        copies_f = [[] for place in f_peers]

        def send_part(step, index):
            here = columns(order[index])
            copy = push(
                made.at[f_peers[step], :, here],
                landed.at[step, :, here],
                send_f.at[step, index],
                recv_f.at[step, index],
                "fsdp",
                f_peers[step],
            )
            copy.start()
            copies_f[step].append(copy)

        compute()
        for index in range(count_c):
            for step in range(rows_f - 1):
                send_part(step, index)
        copies_c = []
        for index, part_place in enumerate(order):
            here = columns(part_place)
            value = made[f_place, :, here].astype(jnp.float32)
            for step in range(rows_f - 1):
                copies_f[step][index].wait_recv()
                value = value + landed[step, :, here].astype(jnp.float32)
            if index < count_c - 1:
                summed[index] = value.astype(jnp.bfloat16)
                copy = push(
                    summed.at[index],
                    landed_c.at[index],
                    send_c.at[index],
                    recv_c.at[index],
                    "ctx",
                    part_place,
                )
                copy.start()
                copies_c.append(copy)
            else:
                total[...] = value
        value = total[...]
        for index, copy in enumerate(copies_c):
            copy.wait_recv()
            value = value + landed_c[index].astype(jnp.float32)
        mine = columns(c_place)
        out[:, mine] = value.astype(jnp.bfloat16)
        copies_g = []
        for index, place in enumerate(c_peers):
            copy = push(
                out.at[:, mine],
                out.at[:, mine],
                send_g.at[index],
                recv_g.at[index],
                "ctx",
                place,
            )
            copy.start()
            copies_g.append(copy)
        for copy in copies_g:
            copy.wait()
        for copy in copies_c:
            copy.wait_send()
        for row in copies_f:
            for copy in row:
                copy.wait_send()


def reduce_grads(active, operands, collective_id):
    rows_f = lax.axis_size("fsdp")
    count_c = lax.axis_size("ctx")
    hid_in, att, hid_mid, grad_y, d_q, d_k, d_v, d_mid, d_gate, d_up, act = operands[:11]
    rows = hid_in.shape[1] // rows_f
    assert att.shape == hid_in.shape
    widths = [d_gate.shape[1], d_up.shape[1], act.shape[1], LANES, LANES]
    widths += [array.shape[1] for array in (d_mid, d_q, d_k, d_v)]
    offsets = [0]
    for width in widths:
        offsets.append(offsets[-1] + padded(width))
    end = offsets.pop()
    part = -(-end // (LANES * count_c)) * LANES
    whole = pl.BlockSpec(memory_space=pltpu.VMEM)
    out = pl.pallas_call(
        functools.partial(
            grads_kernel,
            active,
            rows_f,
            count_c,
            part,
            (tuple(offsets), end),
        ),
        out_shape=jax.ShapeDtypeStruct((rows, count_c * part), jnp.bfloat16),
        in_specs=[whole] * 13,
        out_specs=whole,
        scratch_shapes=[
            pltpu.VMEM((rows_f, rows, count_c * part), jnp.bfloat16),
            pltpu.VMEM((rows_f - 1, rows, count_c * part), jnp.bfloat16),
            pltpu.VMEM((count_c - 1, rows, part), jnp.bfloat16),
            pltpu.VMEM((count_c - 1, rows, part), jnp.bfloat16),
            pltpu.VMEM((rows, part), jnp.float32),
            pltpu.SemaphoreType.DMA((rows_f - 1, count_c)),
            pltpu.SemaphoreType.DMA((rows_f - 1, count_c)),
            pltpu.SemaphoreType.DMA((count_c - 1,)),
            pltpu.SemaphoreType.DMA((count_c - 1,)),
            pltpu.SemaphoreType.DMA((count_c - 1,)),
            pltpu.SemaphoreType.DMA((count_c - 1,)),
        ],
        compiler_params=call_options(collective_id),
        name="reduce_grads",
    )(*operands)
    return out, (offsets, act.shape[1] // rows_f)


def weights_kernel(active, number, held, *refs):
    shards = refs[:number]
    outs = refs[number * (2 if held else 1) :][:number]
    send_sem, recv_sem, own_sem = refs[-3:]
    me = lax.axis_index("fsdp")
    near = me + 1 - 2 * lax.rem(me, 2)
    far = lax.rem(me + 2, 4)

    @pl.when(lax.axis_index("section") == active)
    def run():
        greet([("fsdp", near), ("fsdp", far)])

        def halves(index):
            rows = shards[index].shape[0]
            first = rows // 2 // 16 * 16
            return pl.ds(0, first), pl.ds(first, rows - first)

        def send(index, slot, source, block, rows, place):
            copy = push(
                source,
                outs[index].at[block, rows],
                send_sem.at[index, slot],
                recv_sem.at[index, slot],
                "fsdp",
                place,
            )
            copy.start()
            return copy

        copies = []
        for index in range(number):
            top, low = halves(index)
            copies.append(
                [
                    send(index, 0, shards[index].at[top], me, top, near),
                    send(index, 1, shards[index].at[low], me, low, far),
                    send(index, 2, shards[index].at[low], me, low, near),
                    send(index, 3, shards[index].at[top], me, top, far),
                ]
            )
        locals_ = []
        for index in range(number):
            copy = pltpu.make_async_copy(shards[index], outs[index].at[me], own_sem.at[index])
            copy.start()
            locals_.append(copy)
        for index in range(number):
            top, low = halves(index)
            copies[index][0].wait_recv()
            copies[index].append(send(index, 4, outs[index].at[near, top], near, top, far))
            copies[index][1].wait_recv()
            copies[index].append(send(index, 5, outs[index].at[far, low], far, low, near))
        for index in range(number):
            for slot in range(2, 6):
                copies[index][slot].wait_recv()
            for copy in copies[index]:
                copy.wait_send()
            locals_[index].wait()


def gather_weights(active, shards, held, collective_id):
    count = lax.axis_size("fsdp")
    assert count == 4
    number = len(shards)
    anywhere = pl.BlockSpec(memory_space=pl.ANY)
    operands = tuple(shards) + tuple(held or ())
    return pl.pallas_call(
        functools.partial(weights_kernel, active, number, held is not None),
        out_shape=[jax.ShapeDtypeStruct((count,) + shard.shape, shard.dtype) for shard in shards],
        in_specs=[anywhere] * len(operands),
        out_specs=[anywhere] * number,
        scratch_shapes=[
            pltpu.SemaphoreType.DMA((number, 6)),
            pltpu.SemaphoreType.DMA((number, 6)),
            pltpu.SemaphoreType.DMA((number,)),
        ],
        input_output_aliases={number + index: index for index in range(len(held or ()))},
        compiler_params=call_options(collective_id),
        name="gather_weights",
    )(*operands)


def shifted(array, axis, by):
    devices = lax.axis_size(axis)
    pairs = [(i, i + by) for i in range(devices) if 0 <= i + by < devices]
    return lax.ppermute(array, axis, pairs)


def rope_tables(rope_rows):
    half_width = HEAD // 2
    frequency = THETA ** (-jnp.arange(half_width, dtype=jnp.float32) * (2.0 / HEAD))
    angle = rope_rows.astype(jnp.float32)[:, None] * frequency[None, :]
    return (jnp.cos(angle), jnp.sin(angle))


def rotate(vectors, cosine, sine):
    half_width = vectors.shape[-1] // 2
    front = vectors[..., :half_width]
    second = vectors[..., half_width:]
    cos_rows = cosine[:, None, :]
    sin_rows = sine[:, None, :]
    return jnp.concatenate(
        [front * cos_rows - second * sin_rows, second * cos_rows + front * sin_rows], axis=-1
    )


def normalize(field):
    factor = lax.rsqrt(jnp.mean(field * field, axis=-1, keepdims=True) + EPS)
    return (field * factor, factor)


def norm_back(grad_rows, normed, factor, gain):
    scaled = grad_rows * gain
    back = factor * (scaled - normed * jnp.mean(scaled * normed, axis=-1, keepdims=True))
    return (back, (grad_rows * normed).astype(jnp.bfloat16))


def block_size(row_count):
    return math.gcd(row_count, 512)


def positions_of(span_table, first_row, row_count, shard_rows):
    span_rows = shard_rows // 2
    slot_ids = jnp.arange(span_table.shape[0], dtype=jnp.int32)
    row_ids = first_row + jnp.arange(row_count, dtype=jnp.int32)
    slot_of = 2 * (row_ids // shard_rows) + row_ids % shard_rows // span_rows
    picked = jnp.sum(
        jnp.where(slot_of[:, None] == slot_ids[None, :], span_table[None, :], 0), axis=1
    )
    return picked * span_rows + row_ids % span_rows


def attend_forward(queries, gathered, span_table, local_pos, shard_rows):
    kv_width = gathered.shape[1] // 2
    score_scale = HEAD ** (-0.5)
    total_rows = gathered.shape[0]
    block_rows = block_size(total_rows)
    block_count = total_rows // block_rows
    key_pos = positions_of(span_table, 0, total_rows, shard_rows).reshape(block_count, block_rows)
    blocks = gathered.reshape(block_count, block_rows, gathered.shape[1])

    def masked_scores(kv_block, block_pos):
        key_heads = kv_block[:, :kv_width].reshape(block_rows, KV_HEADS, HEAD)
        scores = (
            jnp.einsum("rkgd,lkd->rkgl", queries, key_heads, preferred_element_type=jnp.float32)
            * score_scale
        )
        allowed = block_pos[None, :] <= local_pos[:, None]
        return jnp.where(allowed[:, None, None, :], scores, -math.inf)

    def total_pass(running, block_item):
        row_top, row_total = running
        scores = masked_scores(block_item[0], block_item[1])
        new_top = jnp.maximum(row_top, jnp.max(scores, axis=-1))
        anchor = jnp.where(new_top == -math.inf, 0.0, new_top)
        row_total = row_total * jnp.exp(row_top - anchor) + jnp.sum(
            jnp.exp(scores - anchor[..., None]), axis=-1
        )
        return ((new_top, row_total), None)

    initial = (
        jnp.full(queries.shape[:3], -math.inf, jnp.float32),
        jnp.zeros(queries.shape[:3], jnp.float32),
    )
    (row_top, row_total), unused = lax.scan(total_pass, initial, (blocks, key_pos))
    log_total = row_top + jnp.log(row_total)

    def value_pass(summed, block_item):
        kv_block, block_pos = block_item
        scores = masked_scores(kv_block, block_pos)
        value_heads = kv_block[:, kv_width:].reshape(block_rows, KV_HEADS, HEAD)
        probs = jnp.exp(scores - log_total[..., None]).astype(jnp.bfloat16)
        summed = summed + jnp.einsum(
            "rkgl,lkd->rkgd", probs, value_heads, preferred_element_type=jnp.float32
        )
        return (summed, None)

    summed, unused = lax.scan(value_pass, jnp.zeros(queries.shape, jnp.float32), (blocks, key_pos))
    return (summed.astype(jnp.bfloat16), log_total)


def attend_backward(
    queries, gathered, span_table, local_pos, log_total, grad_att, row_delta, shard_rows, call_id
):
    kv_width = gathered.shape[1] // 2
    score_scale = HEAD ** (-0.5)
    total_rows = gathered.shape[0]
    block_rows = block_size(total_rows)
    block_count = total_rows // block_rows
    key_pos = positions_of(span_table, 0, total_rows, shard_rows).reshape(block_count, block_rows)
    blocks = gathered.reshape(block_count, block_rows, gathered.shape[1])

    def backward_block(grad_q, block_item):
        kv_block, block_pos = block_item
        key_heads = kv_block[:, :kv_width].reshape(block_rows, KV_HEADS, HEAD)
        value_heads = kv_block[:, kv_width:].reshape(block_rows, KV_HEADS, HEAD)
        scores = (
            jnp.einsum("rkgd,lkd->rkgl", queries, key_heads, preferred_element_type=jnp.float32)
            * score_scale
        )
        allowed = block_pos[None, :] <= local_pos[:, None]
        scores = jnp.where(allowed[:, None, None, :], scores, -math.inf)
        probs = jnp.exp(scores - log_total[..., None])
        grad_v = jnp.einsum(
            "rkgl,rkgd->lkd",
            probs.astype(jnp.bfloat16),
            grad_att,
            preferred_element_type=jnp.float32,
        )
        grad_p = jnp.einsum(
            "rkgd,lkd->rkgl", grad_att, value_heads, preferred_element_type=jnp.float32
        )
        grad_s = (probs * (grad_p - row_delta[..., None])).astype(jnp.bfloat16)
        grad_q = (
            grad_q
            + jnp.einsum("rkgl,lkd->rkgd", grad_s, key_heads, preferred_element_type=jnp.float32)
            * score_scale
        )
        grad_k = (
            jnp.einsum("rkgl,rkgd->lkd", grad_s, queries, preferred_element_type=jnp.float32)
            * score_scale
        )
        joined = jnp.concatenate(
            [grad_k.reshape(block_rows, kv_width), grad_v.reshape(block_rows, kv_width)], axis=1
        )
        return (grad_q, joined)

    grad_q, pieces = lax.scan(
        backward_block, jnp.zeros(queries.shape, jnp.float32), (blocks, key_pos)
    )
    own_grads = collect(pieces.reshape(total_rows, 2 * kv_width), call_id)
    return (grad_q, own_grads)


def forward_layer(layer_input, rope_rows, params, span_table, local_pos, shard_rows, call_id):
    gain_in, w_q, w_k, w_v, w_o, gain_mid, w_g, w_u, w_d = params
    length = layer_input.shape[0]
    residual = layer_input.astype(jnp.float32)
    normed_in, scale_in = normalize(residual)
    hidden_in = (normed_in * gain_in).astype(jnp.bfloat16)
    cosine, sine = rope_tables(rope_rows)
    query = jnp.dot(hidden_in, w_q, preferred_element_type=jnp.float32).reshape(length, -1, HEAD)
    key_proj = jnp.dot(hidden_in, w_k, preferred_element_type=jnp.float32).reshape(
        length, KV_HEADS, HEAD
    )
    value = jnp.dot(hidden_in, w_v, preferred_element_type=jnp.float32).astype(jnp.bfloat16)
    query_b = rotate(query, cosine, sine).astype(jnp.bfloat16).reshape(length, KV_HEADS, -1, HEAD)
    key_b = rotate(key_proj, cosine, sine).astype(jnp.bfloat16).reshape(length, KV_HEADS * HEAD)
    kv_local = spread(jnp.concatenate([key_b, value], axis=1), call_id)
    attended, log_total = attend_forward(query_b, kv_local, span_table, local_pos, shard_rows)
    attended_flat = attended.reshape(length, -1)
    residual_mid = residual + jnp.dot(attended_flat, w_o, preferred_element_type=jnp.float32)
    normed_mid, scale_mid = normalize(residual_mid)
    hidden_mid = (normed_mid * gain_mid).astype(jnp.bfloat16)
    gate_pre = jnp.dot(hidden_mid, w_g, preferred_element_type=jnp.float32)
    up_pre = jnp.dot(hidden_mid, w_u, preferred_element_type=jnp.float32)
    active = (jax.nn.silu(gate_pre) * up_pre).astype(jnp.bfloat16)
    result = residual_mid + jnp.dot(active, w_d, preferred_element_type=jnp.float32)
    saved = (
        normed_in,
        scale_in,
        hidden_in,
        cosine,
        sine,
        query_b,
        kv_local,
        attended,
        log_total,
        normed_mid,
        scale_mid,
        hidden_mid,
        gate_pre,
        up_pre,
        active,
    )
    return (result, saved)


def backward_layer(saved, params, grad_y, span_table, local_pos, shard_rows, call_id):
    gain_in, w_q, w_k, w_v, w_o, gain_mid, w_g, w_u, w_d = params
    (
        normed_in,
        scale_in,
        hidden_in,
        cosine,
        sine,
        query_b,
        kv_local,
        attended,
        log_total,
        normed_mid,
        scale_mid,
        hidden_mid,
        gate_pre,
        up_pre,
        active,
    ) = saved
    length = grad_y.shape[0]
    grad_yb = grad_y.astype(jnp.bfloat16)
    grad_act = jnp.dot(grad_yb, w_d.T, preferred_element_type=jnp.float32)
    sigmoid_gate = jax.nn.sigmoid(gate_pre)
    grad_gate = (grad_act * up_pre * sigmoid_gate * (1.0 + gate_pre * (1.0 - sigmoid_gate))).astype(
        jnp.bfloat16
    )
    grad_up = (grad_act * gate_pre * sigmoid_gate).astype(jnp.bfloat16)
    grad_hmid = jnp.dot(grad_gate, w_g.T, preferred_element_type=jnp.float32) + jnp.dot(
        grad_up, w_u.T, preferred_element_type=jnp.float32
    )
    back_mid, grad_gmid = norm_back(grad_hmid, normed_mid, scale_mid, gain_mid)
    grad_mid = grad_y + back_mid
    grad_midb = grad_mid.astype(jnp.bfloat16)
    attended_flat = attended.reshape(length, -1)
    grad_att = (
        jnp.dot(grad_midb, w_o.T, preferred_element_type=jnp.float32)
        .astype(jnp.bfloat16)
        .reshape(attended.shape)
    )
    row_delta = jnp.sum(grad_att.astype(jnp.float32) * attended.astype(jnp.float32), axis=-1)
    grad_q, grad_kv = attend_backward(
        query_b, kv_local, span_table, local_pos, log_total, grad_att, row_delta, shard_rows, call_id
    )
    kv_width = kv_local.shape[1] // 2
    grad_qraw = (
        rotate(grad_q.reshape(length, -1, HEAD), cosine, -sine)
        .astype(jnp.bfloat16)
        .reshape(length, -1)
    )
    grad_kraw = (
        rotate(grad_kv[:, :kv_width].reshape(length, KV_HEADS, HEAD), cosine, -sine)
        .astype(jnp.bfloat16)
        .reshape(length, kv_width)
    )
    grad_vb = grad_kv[:, kv_width:].astype(jnp.bfloat16)
    grad_hin = (
        jnp.dot(grad_qraw, w_q.T, preferred_element_type=jnp.float32)
        + jnp.dot(grad_kraw, w_k.T, preferred_element_type=jnp.float32)
        + jnp.dot(grad_vb, w_v.T, preferred_element_type=jnp.float32)
    )
    back_in, grad_gin = norm_back(grad_hin, normed_in, scale_in, gain_in)
    grad_entry = grad_mid + back_in
    return (
        grad_entry,
        (
            hidden_in,
            attended_flat,
            hidden_mid,
            grad_yb,
            grad_qraw,
            grad_kraw,
            grad_vb,
            grad_midb,
            grad_gate,
            grad_up,
            active,
            grad_gin,
            grad_gmid,
        ),
    )


def body(
    block_input,
    cotangent,
    span_order,
    rope_ids,
    norm_in,
    w_query,
    w_key,
    w_value,
    w_out,
    norm_mid,
    w_gate,
    w_up,
    w_down,
):
    micro_count = block_input.shape[0]
    shard_rows = block_input.shape[2]
    ctx_place = lax.axis_index("ctx")
    leading = lax.axis_index("section") == 0
    local_pos = positions_of(span_order, ctx_place * shard_rows, shard_rows, shard_rows)
    shards = (w_query[0], w_key[0], w_value[0], w_out[0], w_gate[0], w_up[0], w_down[0])
    held = gather_weights(0, shards, None, 6)

    def params_of(blocks):
        full = [block.reshape((-1, block.shape[2])) for block in blocks]
        return (norm_in[0], *full[:4], norm_mid[0], *full[4:])

    params = params_of(held)
    received = jnp.zeros(block_input.shape[2:], jnp.bfloat16)
    kept_states = []
    outputs = []
    for tick_index in range(micro_count + 1):
        fresh_rows = block_input[min(tick_index, micro_count - 1), 0]
        layer_input = jnp.where(leading, fresh_rows, received)
        rope_rows = jnp.where(
            leading,
            rope_ids[min(tick_index, micro_count - 1), 0],
            rope_ids[max(tick_index - 1, 0), 0],
        )
        result, saved = forward_layer(
            layer_input, rope_rows, params, span_order, local_pos, shard_rows, tick_index
        )
        sent_rows = result.astype(jnp.bfloat16)
        kept_states.append(saved)
        outputs.append(sent_rows)
        if tick_index < micro_count:
            sent_rows, held = lax.optimization_barrier((sent_rows, tuple(held)))
            held = gather_weights(1, shards, held, 7)
            sent_rows, held = lax.optimization_barrier((sent_rows, tuple(held)))
            params = params_of(held)
            received = shifted(sent_rows, "section", 1)
    returned = jnp.zeros(block_input.shape[2:], jnp.bfloat16)
    reduced = []
    grad_inputs = []
    for tick_index in range(micro_count + 1):
        if tick_index < micro_count:
            fresh_rows = cotangent[tick_index, 0]
        else:
            fresh_rows = jnp.zeros_like(cotangent[0, 0])
        arrival = jnp.where(leading, returned, fresh_rows).astype(jnp.float32)
        saved = jax.tree.map(
            lambda left, right: jnp.where(leading, left, right),
            kept_states[max(tick_index - 1, 0)],
            kept_states[min(tick_index + 1, micro_count)],
        )
        grad_entry, terms = backward_layer(
            saved, params, arrival, span_order, local_pos, shard_rows, 2 + tick_index
        )
        grad_inputs.append(grad_entry)
        if tick_index < micro_count:
            returned = shifted(grad_entry.astype(jnp.bfloat16), "section", -1)
        share, places = reduce_grads(1 - tick_index, terms, 4 + tick_index)
        reduced.append(share)
    layer_out = jnp.stack([jnp.where(leading, outputs[0], outputs[1])])
    grad_in = jnp.stack([jnp.where(leading, grad_inputs[1], grad_inputs[0])])
    layer_out = layer_out.reshape((1, micro_count, 1) + layer_out.shape[1:])
    grad_in = grad_in.reshape((1, micro_count, 1) + grad_in.shape[1:])
    share = jnp.where(leading, reduced[1], reduced[0]).astype(jnp.float32)
    offsets, act_cols = places

    def cut(first, width):
        return share[:, first : first + width]

    q_width, kv_width, ff_width = w_query.shape[2], w_key.shape[2], w_gate.shape[2]
    rows = share.shape[0]
    down_parts = block_input.shape[3] // rows
    grad_down = cut(offsets[2], down_parts * act_cols).reshape(rows, down_parts, act_cols)
    grad_down = grad_down.transpose(2, 1, 0).reshape(act_cols, down_parts * rows)
    totals = (
        cut(offsets[3], 1)[:, 0],
        cut(offsets[6], q_width),
        cut(offsets[7], kv_width),
        cut(offsets[8], kv_width),
        cut(offsets[5], block_input.shape[3]),
        cut(offsets[4], 1)[:, 0],
        cut(offsets[0], ff_width),
        cut(offsets[1], ff_width),
        grad_down,
    )
    return (layer_out, grad_in) + tuple((summed_part[None] for summed_part in totals))


def solution(mesh):
    placed = (
        P(None, "fsdp", "ctx", None),
        P(None, "fsdp", "ctx", None),
        P(),
        P(None, "fsdp", "ctx"),
        P("section", None),
        P("section", "fsdp", None),
        P("section", "fsdp", None),
        P("section", "fsdp", None),
        P("section", "fsdp", None),
        P("section", None),
        P("section", "fsdp", None),
        P("section", "fsdp", None),
        P("section", "fsdp", None),
    )
    return jax.shard_map(
        body,
        mesh=mesh,
        in_specs=placed,
        out_specs=(
            P("section", None, "fsdp", "ctx", None),
            P("section", None, "fsdp", "ctx", None),
            P("section", "fsdp"),
            P("section", "fsdp", None),
            P("section", "fsdp", None),
            P("section", "fsdp", None),
            P("section", "fsdp", None),
            P("section", "fsdp"),
            P("section", "fsdp", None),
            P("section", "fsdp", None),
            P("section", "fsdp", None),
        ),
        check_vma=False,
    )
```
